512 devices in a mesh: rep: 32 (over x, z_lo, core), fsdp: 16 (over y, z_hi).
Axes of the slice: x: 4, y: 8, z: 8 (z_hi: 2, z_lo: 4; z = z_hi * 4 + z_lo), core: 2. Of those that a mesh axis runs over, the one named last changes fastest.
Arguments:
- activations: bfloat16 [32, 4096, 4608], P('rep', 'fsdp'), may hold values from -6 to 6
- weights: float32 [32, 4608, 384], P('rep', 'fsdp'), may hold values from -8 to 8
- momentum: float32 [32, 4608, 384], P('rep', 'fsdp'), may hold values from -3 to 3
- cotangent: bfloat16 [32, 4096, 128], P('rep', 'fsdp'), may hold values from -6 to 6
- step: int32 [1], replicated, may hold values from 0 to 63
Outputs:
- new_weights: float32 [32, 4608, 384], P('rep', 'fsdp')
- new_momentum: float32 [32, 4608, 384], P('rep', 'fsdp')
The draws below stay inside these ranges and needn't reach their ends.
All inputs are finite; a program needn't handle non-finite values.
Results may differ from the reference program's by a relative error of at most 0.023.
Values may be sent and summed in bfloat16 or wider, within the bound.
A program may use at most 64 MiB of HBM per device.

```python
import jax
import jax.numpy as jnp
from jax import lax

D = 4608
HEADS = 32
HEAD = 128
TOKENS = 4096
REPLICAS = 32
PERIOD = 4
N_FSDP = 16


def draw_weights(key, part):
    key = jax.random.fold_in(key, 11)
    shape = (REPLICAS, D, 3 * HEAD)
    values = jnp.clip(1.4 * jax.random.normal(key, shape, jnp.float32), -8.0, 8.0)
    return values


def block_scale(key, shape, shards, smallest, top_value):
    gain = 1.0
    for axis_at, shards_of in shards:
        draws = jax.random.uniform(jax.random.fold_in(jax.random.fold_in(key, 6), axis_at), (shards_of,), jnp.float32, smallest / len(shards), top_value / len(shards))
        gain = gain * jnp.repeat(jnp.exp(draws), shape[axis_at] // shards_of).reshape((-1,) + (1,) * (len(shape) - 1 - axis_at))
    return gain


def noise(key, extent, deviation, bound, split=(), kind=jnp.bfloat16):
    values = deviation * jax.random.normal(key, extent, jnp.float32)
    if split:
        values = values * block_scale(key, extent, split, -0.22, 0.18)
    return jnp.clip(values, -bound, bound).astype(kind)


def setup_inputs(seed: int = 0) -> dict:
    arg_keys = jax.random.split(jax.random.key(seed), 6)
    return {
        "activations": noise(arg_keys[0], (REPLICAS, TOKENS, D), 1.0, 6.0, ((0, 32), (1, 16))),
        "weights": draw_weights(jax.random.fold_in(arg_keys[5], 71), 0),
        "momentum": noise(arg_keys[2], (REPLICAS, D, 3 * HEAD), 0.5, 3.0, ((0, 32), (1, 16)), jnp.float32),
        "cotangent": noise(arg_keys[3], (REPLICAS, TOKENS, HEAD), 1.0, 6.0, ((0, 32), (1, 16))),
        "step": jax.random.randint(arg_keys[4], (1,), 0, 64).astype(jnp.int32),
    }


SOFT_CAP = 50.0
ROPE_BASE = 10000.0
MOMENTUM_DECAY = 0.9
LEARNING_RATE = 0.5


def rotate(matrix, positions, direction):
    half = matrix.shape[1] // 2
    freqs = ROPE_BASE ** (-(jnp.arange(half, dtype=jnp.float32) * 2.0 / matrix.shape[1]))
    angles = positions[:, None] * freqs[None, :]
    cosine = jnp.cos(angles)
    sine = jnp.sin(angles)
    first = matrix[:, :half]
    second = matrix[:, half:]
    return jnp.concatenate([first * cosine - direction * second * sine, second * cosine + direction * first * sine], axis=1)


def one_replica(operands):
    acts, params, moment, grad_out = operands
    tokens_all = acts.shape[0]
    width = acts.shape[1]
    head_size = grad_out.shape[1]
    qscale = float(width // HEADS) ** -0.5
    positions = jnp.arange(tokens_all, dtype=jnp.float32)
    index_row = jnp.arange(tokens_all, dtype=jnp.int32)
    proj = jnp.dot(acts, params.astype(jnp.bfloat16), preferred_element_type=jnp.float32) * float(width) ** -0.5
    query_rot = rotate(proj[:, :head_size], positions, 1.0).astype(jnp.bfloat16)
    key_rot = rotate(proj[:, head_size:2 * head_size], positions, 1.0).astype(jnp.bfloat16)
    values = proj[:, 2 * head_size:].astype(jnp.bfloat16)
    raw = jnp.dot(query_rot, key_rot.T, preferred_element_type=jnp.float32) * qscale
    tangent = jnp.tanh(raw / SOFT_CAP)
    causal = index_row[:, None] >= index_row[None, :]
    expo = jnp.where(causal, jnp.exp(SOFT_CAP * tangent), jnp.float32(0.0))
    row_total = jnp.sum(expo, axis=1)
    output = (jnp.dot(expo.astype(jnp.bfloat16), values, preferred_element_type=jnp.float32) / row_total[:, None]).astype(jnp.bfloat16)
    prob = expo / row_total[:, None]
    dvalues = jnp.dot(prob.astype(jnp.bfloat16).T, grad_out, preferred_element_type=jnp.float32).astype(jnp.bfloat16)
    delta = jnp.sum(grad_out.astype(jnp.float32) * output.astype(jnp.float32), axis=1)
    dprob = jnp.dot(grad_out, values.T, preferred_element_type=jnp.float32)
    dscore = (prob * (dprob - delta[:, None]) * (1.0 - tangent * tangent) * qscale).astype(jnp.bfloat16)
    dquery = rotate(jnp.dot(dscore, key_rot, preferred_element_type=jnp.float32), positions, -1.0)
    dkey = rotate(jnp.dot(dscore.T, query_rot, preferred_element_type=jnp.float32), positions, -1.0)
    dproj = jnp.concatenate([dquery.astype(jnp.bfloat16), dkey.astype(jnp.bfloat16), dvalues], axis=1)
    act_blocks = acts.reshape(N_FSDP, tokens_all // N_FSDP, width).astype(jnp.float32)
    grad_blocks = dproj.reshape(N_FSDP, tokens_all // N_FSDP, 3 * head_size).astype(jnp.float32)
    terms = jnp.einsum("btr,btc->brc", act_blocks, grad_blocks) * float(width) ** -0.5
    grad = jnp.sum(terms.astype(jnp.bfloat16).astype(jnp.float32), axis=0)
    new_moment = MOMENTUM_DECAY * moment + grad
    stepped = params - LEARNING_RATE * new_moment
    return stepped, new_moment


def reference(activations, weights, momentum, cotangent, step):
    stepped, new_momentum = lax.map(one_replica, (activations, weights, momentum, cotangent))
    distance = jnp.left_shift(jnp.int32(1), (step[0] % PERIOD).astype(jnp.int32))
    partner = jnp.roll(stepped, distance, axis=0)
    new_weights = (stepped + partner) * 0.5
    return new_weights, new_momentum
```

```python
import functools

import jax
import jax.numpy as jnp
import numpy as np
from jax import lax
from jax.experimental import pallas as pl
from jax.experimental.pallas import tpu as pltpu
from jax.sharding import PartitionSpec as P

HEADS = 32
PERIOD = 4
SOFT_CAP = 50.0
ROPE_BASE = 10000.0
MOMENTUM_DECAY = 0.9
LEARNING_RATE = 0.5
RING = 8
BF16 = jnp.bfloat16
F32 = jnp.float32
MESH = pl.DeviceIdType.MESH


def dot_nn(left, right):
    return lax.dot_general(left, right, (((1,), (0,)), ((), ())), preferred_element_type=F32)


def dot_nt(left, right):
    return lax.dot_general(left, right, (((1,), (1,)), ((), ())), preferred_element_type=F32)


def dot_tn(left, right):
    return lax.dot_general(left, right, (((0,), (0,)), ((), ())), preferred_element_type=F32)


def hops_of(direction, half):
    return RING // 2 if half == direction else RING // 2 - 1


class Gather:
    def __init__(self, buffer, rows, place, send_sem, recv_sem, base, y, device):
        self.buffer, self.rows, self.place = buffer, rows, place
        self.send_sem, self.recv_sem, self.base = send_sem, recv_sem, base
        self.y, self.device = y, device

    def copy(self, hop, direction, half, arriving):
        sign = 1 if direction == 0 else RING - 1
        back = hop if arriving else hop - 1
        source = lax.rem(self.y + (RING - sign) * back, RING)
        part = self.rows // 2
        start = pl.multiple_of(self.place(source) + half * part, 16)
        view = self.buffer.at[pl.ds(start, part), :]
        slot = self.base + ((hop - 1) * 2 + direction) * 2 + half
        return pltpu.make_async_remote_copy(
            src_ref=view,
            dst_ref=view,
            send_sem=self.send_sem.at[slot],
            recv_sem=self.recv_sem.at[slot],
            device_id=self.device(lax.rem(self.y + sign, RING)),
            device_id_type=MESH,
        )

    def units(self, hop):
        order = [(0, 0), (1, 1), (0, 1), (1, 0)]
        return [(d, h) for d, h in order if 1 <= hop <= hops_of(d, h)]

    def start(self):
        for direction, half in self.units(1):
            self.copy(1, direction, half, False).start()

    def relay(self, hop):
        for direction, half in self.units(hop):
            self.copy(hop, direction, half, True).wait_recv()
            if hop < hops_of(direction, half):
                self.copy(hop + 1, direction, half, False).start()

    def drain(self):
        for hop in range(1, RING // 2 + 1):
            for direction, half in self.units(hop):
                self.copy(hop, direction, half, False).wait_send()


class Scatter:
    def __init__(self, own, outgoing, incoming, send_sem, recv_sem, base, y, device):
        self.own, self.outgoing, self.incoming = own, outgoing, incoming
        self.send_sem, self.recv_sem, self.base = send_sem, recv_sem, base
        self.y, self.device = y, device

    def copy(self, step, direction, half):
        sign = 1 if direction == 0 else RING - 1
        index = (step * 2 + direction) * 2 + half
        return pltpu.make_async_remote_copy(
            src_ref=self.outgoing.at[index],
            dst_ref=self.incoming.at[index],
            send_sem=self.send_sem.at[self.base + index],
            recv_sem=self.recv_sem.at[self.base + index],
            device_id=self.device(lax.rem(self.y + sign, RING)),
            device_id_type=MESH,
        )

    def units(self, step):
        order = [(0, 0), (1, 1), (0, 1), (1, 0)]
        return [(d, h) for d, h in order if RING // 2 - step <= hops_of(d, h)]

    def step(self, step):
        for direction, half in self.units(step):
            sign = 1 if direction == 0 else RING - 1
            target = lax.rem(self.y + sign * (RING // 2 - step), RING)
            total = self.own(target, half)
            if step > 0 and (direction, half) in self.units(step - 1):
                self.copy(step - 1, direction, half).wait_recv()
                total += self.incoming[((step - 1) * 2 + direction) * 2 + half].astype(F32)
            self.outgoing[(step * 2 + direction) * 2 + half] = total.astype(BF16)
            self.copy(step, direction, half).start()

    def result(self, half):
        last = RING // 2 - 1
        total = self.own(self.y, half)
        for direction in range(2):
            self.copy(last, direction, half).wait_recv()
            total += self.incoming[(last * 2 + direction) * 2 + half].astype(F32)
        return total

    def drain(self):
        for step in range(RING // 2):
            for direction, half in self.units(step):
                self.copy(step, direction, half).wait_send()


W_OWN, W_PAIR, DOUT, QUERY, DQUERY, G_PAIR, G_OWN = range(0, 7 * 16, 16)
Z_W, Z_KV, Z_DKV, Z_G = 112, 114, 116, 118
STATS = 120
SEMS = 128


def kernel(
    acts_hbm,
    weights_ref,
    momentum_hbm,
    dout_ref,
    near_ref,
    far_ref,
    new_momentum_ref,
    stepped_ref,
    acts,
    acts_t,
    momentum,
    wall,
    dout_all,
    query_all,
    kv_all,
    expo_buf,
    slope_buf,
    dprob_buf,
    stats_own,
    stats_in,
    dq_buf,
    dq_out,
    dq_in,
    dkv_acc,
    dkv_out,
    dkv_in,
    dproj,
    g_out_pair,
    g_in_pair,
    g_out_own,
    g_in_own,
    z_out,
    z_in,
    send_sem,
    recv_sem,
    local_sem,
):
    rows = weights_ref.shape[0]
    tokens, head = dout_ref.shape
    width = acts.shape[1]
    qscale = float(width // HEADS) ** (-0.5)
    pscale = float(width) ** (-0.5)

    place = lax.axis_index("fsdp")
    y = lax.div(place, 2)
    zh = lax.rem(place, 2)

    def column(row):
        return {"fsdp": row * 2 + zh}

    pair = {"fsdp": y * 2 + (1 - zh)}

    acts_copy = pltpu.make_async_copy(acts_hbm, acts, local_sem.at[0])
    acts_copy.start()
    momentum_copy = pltpu.make_async_copy(momentum_hbm, momentum, local_sem.at[1])
    momentum_copy.start()

    barrier = pltpu.get_barrier_semaphore()
    for ahead in range(1, RING):
        pl.semaphore_signal(
            barrier, inc=1, device_id=column(lax.rem(y + ahead, RING)), device_id_type=MESH
        )
    pl.semaphore_signal(barrier, inc=1, device_id=pair, device_id_type=MESH)

    wall[pl.ds(pl.multiple_of(place * rows, 16), rows), :] = weights_ref[...].astype(BF16)
    dout_all[pl.ds(pl.multiple_of(y * tokens, 16), tokens), :] = dout_ref[...]
    pl.semaphore_wait(barrier, RING)

    def pair_copy(source, target, slot):
        return pltpu.make_async_remote_copy(
            src_ref=source,
            dst_ref=target,
            send_sem=send_sem.at[slot],
            recv_sem=recv_sem.at[slot],
            device_id=pair,
            device_id_type=MESH,
        )

    def w_view(z, half):
        start = (y * 2 + z) * rows + half * (rows // 2)
        return wall.at[pl.ds(pl.multiple_of(start, 16), rows // 2), :]

    own = Gather(wall, rows, lambda s: (s * 2 + zh) * rows, send_sem, recv_sem, W_OWN, y, column)
    other = Gather(
        wall, rows, lambda s: (s * 2 + (1 - zh)) * rows, send_sem, recv_sem, W_PAIR, y, column
    )
    douts = Gather(dout_all, tokens, lambda s: s * tokens, send_sem, recv_sem, DOUT, y, column)

    tile = 128
    tiles = width // tile
    turned = 0

    def turn(until):
        nonlocal turned
        until = min(until, tiles)
        if until <= turned:
            return

        @pl.loop(turned, until)
        def _(t):
            at = pl.multiple_of(t * tile, tile)
            acts_t[pl.ds(at, tile), :] = acts[:, pl.ds(at, tile)].T

        turned = until

    for half in range(2):
        pair_copy(w_view(zh, half), w_view(zh, half), Z_W + half).start()
    own.start()
    douts.start()
    acts_copy.wait()
    turn(3)
    own.relay(1)
    turn(6)
    douts.relay(1)
    turn(9)
    for half in range(2):
        pair_copy(w_view(zh, half), w_view(1 - zh, half), Z_W + half).wait_recv()
    other.start()
    own.relay(2)
    turn(14)
    other.relay(1)
    douts.relay(2)
    turn(19)
    own.relay(3)
    turn(24)
    other.relay(2)
    douts.relay(3)
    turn(30)
    own.relay(4)
    other.relay(3)
    turn(tiles)
    douts.relay(4)
    other.relay(4)

    near_cos, near_sin = near_ref[0], near_ref[1]
    far_cos = far_ref[0, pl.ds(place, 1), :]
    far_sin = far_ref[1, pl.ds(place, 1), :]
    cosine = near_cos * far_cos - near_sin * far_sin
    sine = near_sin * far_cos + near_cos * far_sin
    half_head = head // 2
    lane = lax.broadcasted_iota(jnp.int32, (tokens, head), 1)
    signed = jnp.where(lane < half_head, -sine, sine)

    def turned_by(matrix, direction):
        return matrix * cosine + direction * pltpu.roll(matrix, half_head, 1) * signed

    proj = dot_nn(acts[...], wall[...]) * pscale
    here = pl.ds(pl.multiple_of(y * tokens, 16), tokens)
    mine = pl.ds(pl.multiple_of(zh * tokens, 16), tokens)
    query_all[here, :] = turned_by(proj[:, :head], 1.0).astype(BF16)
    queries = Gather(
        query_all, tokens, lambda s: s * tokens, send_sem, recv_sem, QUERY, y, column
    )
    queries.start()
    kv_all[mine, :head] = turned_by(proj[:, head : 2 * head], 1.0).astype(BF16)
    kv_all[mine, head:] = proj[:, 2 * head :].astype(BF16)
    theirs = pl.ds(pl.multiple_of((1 - zh) * tokens, 16), tokens)
    pair_copy(kv_all.at[mine, :], kv_all.at[mine, :], Z_KV).start()
    stats_own[...] = jnp.zeros_like(stats_own)
    for hop in range(1, RING // 2 + 1):
        queries.relay(hop)
    pair_copy(kv_all.at[mine, :], kv_all.at[theirs, :], Z_KV).wait_recv()

    sub = min(128, 2 * tokens)

    @pl.loop(y, RING)
    def _(block):
        at = pl.ds(pl.multiple_of(block * tokens, 16), tokens)
        query = query_all[at, :]
        dout = dout_all[at, :]
        total = jnp.zeros((1, tokens), F32)
        cross = jnp.zeros((1, tokens), F32)
        for part in range(0, 2 * tokens, sub):
            score = dot_nt(kv_all[part : part + sub, :head], query)
            dprob = dot_nt(kv_all[part : part + sub, head:], dout)
            tangent = jnp.tanh(score * (qscale / SOFT_CAP))
            key_at = lax.broadcasted_iota(jnp.int32, (sub, tokens), 0) + part
            query_at = lax.broadcasted_iota(jnp.int32, (sub, tokens), 1)
            keep = key_at - query_at <= (block - y) * (2 * tokens) + zh * tokens
            expo = jnp.where(keep, jnp.exp(SOFT_CAP * tangent), 0.0)
            expo_buf[block, part : part + sub, :] = expo
            slope_buf[block, part : part + sub, :] = expo * (1.0 - tangent * tangent)
            dprob_buf[block, part : part + sub, :] = dprob
            total += jnp.sum(expo, axis=0, keepdims=True)
            cross += jnp.sum(expo * dprob, axis=0, keepdims=True)
        stats_own[pl.ds(block, 1), :] = total
        stats_own[pl.ds(block + RING, 1), :] = cross

    def stats_copy(ahead):
        return pltpu.make_async_remote_copy(
            src_ref=stats_own,
            dst_ref=stats_in.at[ahead],
            send_sem=send_sem.at[STATS + ahead],
            recv_sem=recv_sem.at[STATS + ahead],
            device_id=column(lax.rem(y + ahead, RING)),
            device_id_type=MESH,
        )

    for ahead in range(1, RING):
        stats_copy(ahead).start()
    dq_buf[...] = jnp.zeros_like(dq_buf)
    dkv_acc[...] = jnp.zeros_like(dkv_acc)
    stats = stats_own[...]
    for ahead in range(1, RING):
        stats_copy(ahead).wait_recv()
        stats += stats_in[ahead]
    for ahead in range(1, RING):
        stats_copy(ahead).wait_send()
    inverse = 1.0 / stats[:RING, :]
    stats_own[:RING, :] = inverse
    stats_own[RING:, :] = stats[RING:, :] * inverse

    @pl.loop(y, RING)
    def _(block):
        at = pl.ds(pl.multiple_of(block * tokens, 16), tokens)
        query = query_all[at, :]
        dout = dout_all[at, :]
        inv = stats_own[pl.ds(block, 1), :]
        delta = stats_own[pl.ds(block + RING, 1), :]
        dquery = jnp.zeros((tokens, head), F32)
        for part in range(0, 2 * tokens, sub):
            span = slice(part, part + sub)
            prob = (expo_buf[block, span, :] * inv).astype(BF16)
            dscore = (
                slope_buf[block, span, :] * (dprob_buf[block, span, :] - delta) * (inv * qscale)
            ).astype(BF16)
            dkv_acc[span, :head] += dot_nn(dscore, query)
            dkv_acc[span, head:] += dot_nn(prob, dout)
            dquery += dot_tn(dscore, kv_all[span, :head])
        dq_buf[at, :] = dquery

    dkv_out[...] = dkv_acc[theirs, :].astype(BF16)
    dkv_copy = pair_copy(dkv_out, dkv_in, Z_DKV)
    dkv_copy.start()

    def dq_own(target, half):
        start = target * tokens + half * (tokens // 2)
        return dq_buf[pl.ds(pl.multiple_of(start, 16), tokens // 2), :]

    dqueries = Scatter(dq_own, dq_out, dq_in, send_sem, recv_sem, DQUERY, y, column)
    for step in range(RING // 2):
        dqueries.step(step)
    dkv_copy.wait_recv()
    dkv = dkv_acc[mine, :] + dkv_in[...].astype(F32)
    dproj[:, head : 2 * head] = turned_by(dkv[:, :head], -1.0).astype(BF16)
    dproj[:, 2 * head :] = dkv[:, head:].astype(BF16)
    dquery = jnp.concatenate([dqueries.result(0), dqueries.result(1)], axis=0)
    dproj[:, :head] = turned_by(dquery, -1.0).astype(BF16)

    def g_term(z):
        def term(target, half):
            start = (target * 2 + z) * rows + half * (rows // 2)
            block = acts_t[pl.ds(pl.multiple_of(start, 16), rows // 2), :]
            return dot_nn(block, dproj[...]) * pscale

        return term

    g_pair = Scatter(
        g_term(1 - zh), g_out_pair, g_in_pair, send_sem, recv_sem, G_PAIR, y, column
    )
    g_own = Scatter(g_term(zh), g_out_own, g_in_own, send_sem, recv_sem, G_OWN, y, column)
    g_pair.step(0)
    g_pair.step(1)
    g_own.step(0)
    g_pair.step(2)
    g_own.step(1)
    g_pair.step(3)
    g_own.step(2)
    for half in range(2):
        z_out[half] = g_pair.result(half).astype(BF16)
        pair_copy(z_out.at[half], z_in.at[half], Z_G + half).start()
    g_own.step(3)
    momentum_copy.wait()
    for half in range(2):
        grad = g_own.result(half)
        pair_copy(z_out.at[half], z_in.at[half], Z_G + half).wait_recv()
        grad += z_in[half].astype(F32)
        span = slice(half * (rows // 2), (half + 1) * (rows // 2))
        moved = MOMENTUM_DECAY * momentum[span, :] + grad
        new_momentum_ref[span, :] = moved
        stepped_ref[span, :] = weights_ref[span, :] - LEARNING_RATE * moved

    for gather in (own, other, douts, queries):
        gather.drain()
    for scatter in (dqueries, g_pair, g_own):
        scatter.drain()
    for half in range(2):
        pair_copy(w_view(zh, half), w_view(zh, half), Z_W + half).wait_send()
        pair_copy(z_out.at[half], z_in.at[half], Z_G + half).wait_send()
    pair_copy(kv_all.at[mine, :], kv_all.at[mine, :], Z_KV).wait_send()
    dkv_copy.wait_send()


def rope_tables(tokens, places, head):
    half = head // 2
    freqs = ROPE_BASE ** (-(np.arange(half, dtype=np.float64) * 2.0 / head))
    freqs = np.concatenate([freqs, freqs])
    near = np.arange(tokens, dtype=np.float64)[:, None] * freqs
    far = (np.arange(places, dtype=np.float64) * tokens)[:, None] * freqs
    return (
        np.stack([np.cos(near), np.sin(near)]).astype(np.float32),
        np.stack([np.cos(far), np.sin(far)]).astype(np.float32),
    )


def passed_along(value, axis, steps):
    count = lax.axis_size(axis)
    pairs = [(source, (source + steps) % count) for source in range(count)]
    return lax.ppermute(value, axis, pairs)


def on_device(activations, weights, momentum, cotangent, step):
    acts = activations[0]
    params = weights[0]
    moment = momentum[0]
    dout = cotangent[0]
    tokens, width = acts.shape
    rows, columns = params.shape
    head = dout.shape[1]
    places = lax.axis_size("fsdp")
    near, far = rope_tables(tokens, places, head)
    vmem = pl.BlockSpec(memory_space=pltpu.VMEM)
    anywhere = pl.BlockSpec(memory_space=pl.ANY)
    steps = 16
    new_moment, stepped = pl.pallas_call(
        kernel,
        out_shape=[jax.ShapeDtypeStruct((rows, columns), F32)] * 2,
        in_specs=[anywhere, vmem, anywhere, vmem, vmem, vmem],
        out_specs=[vmem, vmem],
        scratch_shapes=[
            pltpu.VMEM((tokens, width), BF16),
            pltpu.VMEM((width, tokens), BF16),
            pltpu.VMEM((rows, columns), F32),
            pltpu.VMEM((width, columns), BF16),
            pltpu.VMEM((RING * tokens, head), BF16),
            pltpu.VMEM((RING * tokens, head), BF16),
            pltpu.VMEM((2 * tokens, 2 * head), BF16),
            pltpu.VMEM((RING, 2 * tokens, tokens), F32),
            pltpu.VMEM((RING, 2 * tokens, tokens), F32),
            pltpu.VMEM((RING, 2 * tokens, tokens), F32),
            pltpu.VMEM((2 * RING, tokens), F32),
            pltpu.VMEM((RING, 2 * RING, tokens), F32),
            pltpu.VMEM((RING * tokens, head), F32),
            pltpu.VMEM((steps, tokens // 2, head), BF16),
            pltpu.VMEM((steps, tokens // 2, head), BF16),
            pltpu.VMEM((2 * tokens, 2 * head), F32),
            pltpu.VMEM((tokens, 2 * head), BF16),
            pltpu.VMEM((tokens, 2 * head), BF16),
            pltpu.VMEM((tokens, columns), BF16),
            pltpu.VMEM((steps, rows // 2, columns), BF16),
            pltpu.VMEM((steps, rows // 2, columns), BF16),
            pltpu.VMEM((steps, rows // 2, columns), BF16),
            pltpu.VMEM((steps, rows // 2, columns), BF16),
            pltpu.VMEM((2, rows // 2, columns), BF16),
            pltpu.VMEM((2, rows // 2, columns), BF16),
            pltpu.SemaphoreType.DMA((SEMS,)),
            pltpu.SemaphoreType.DMA((SEMS,)),
            pltpu.SemaphoreType.DMA((2,)),
        ],
        compiler_params=pltpu.CompilerParams(
            collective_id=0, has_side_effects=True, vmem_limit_bytes=56 * 2**20
        ),
        name="attention_step",
    )(acts, params, moment, dout, jnp.asarray(near), jnp.asarray(far))
    replicas = lax.axis_size("rep")
    branches = [
        functools.partial(
            lambda by, value: passed_along(value.astype(BF16), "rep", by).astype(F32),
            2**level % replicas,
        )
        for level in range(PERIOD)
    ]
    partner = lax.switch(step[0] % PERIOD, branches, stepped)
    new_weights = (stepped + partner) * 0.5
    return (new_weights[None], new_moment[None])


def solution(mesh):
    spec = P("rep", "fsdp", None)
    return jax.shard_map(
        on_device,
        mesh=mesh,
        in_specs=(spec, spec, spec, spec, P()),
        out_specs=(spec, spec),
        check_vma=False,
    )
```

```python
import functools

import jax
import jax.numpy as jnp
import numpy as np
from jax import lax
from jax.experimental import pallas as pl
from jax.experimental.pallas import tpu as pltpu
from jax.sharding import PartitionSpec as P

HEADS = 32
PERIOD = 4
SOFT_CAP = 50.0
ROPE_BASE = 10000.0
MOMENTUM_DECAY = 0.9
LEARNING_RATE = 0.5
RING = 8
FAR = RING // 2
BF16 = jnp.bfloat16
F32 = jnp.float32
MESH = pl.DeviceIdType.MESH
SEMS = 192
OFFSETS = (4, 3, 5, 2, 6, 1, 7, 0)
GROUPS = ((0, 3), (3, 5), (5, 8))

GATHER_ORDER = (
    1, 27, 0, 91, 99, 51, 2, 101, 94, 92, 93, 50, 97, 52, 26, 100, 103, 102, 96, 95,
    75, 76, 98, 25, 3, 29, 19, 9, 4, 17, 28, 18, 10, 67, 69, 59, 54, 42, 34, 20,
    35, 46, 11, 21, 6, 68, 5, 45, 12, 43, 61, 71, 60, 44, 36, 37, 13, 31, 23, 53,
    22, 14, 7, 8, 30, 62, 15, 56, 38, 48, 70, 33, 55, 16, 24, 39, 63, 47, 64, 77,
    73, 58, 32, 49, 78, 40, 104, 85, 41, 72, 86, 74, 65, 57, 66, 79, 80, 105, 106, 83,
    84, 89, 88, 107, 108, 87, 90, 81, 82,
)
SCATTER_ORDER = (
    3, 2, 77, 1, 0, 7, 6, 8, 11, 12, 23, 16, 15, 13, 9, 33, 5, 4, 34, 35,
    38, 45, 18, 37, 36, 17, 24, 25, 14, 46, 10, 40, 55, 60, 59, 20, 56, 39, 26, 67,
    57, 19, 48, 27, 58, 62, 61, 42, 41, 68, 21, 22, 47, 28, 63, 64, 69, 70, 31, 43,
    44, 49, 50, 65, 66, 71, 72, 53, 29, 30, 51, 52, 75, 73, 74, 32, 54, 76,
)


def dot_nn(left, right):
    return lax.dot_general(left, right, (((1,), (0,)), ((), ())), preferred_element_type=F32)


def dot_nt(left, right):
    return lax.dot_general(left, right, (((1,), (1,)), ((), ())), preferred_element_type=F32)


def dot_tn(left, right):
    return lax.dot_general(left, right, (((0,), (0,)), ((), ())), preferred_element_type=F32)


def aligned(start):
    return start if isinstance(start, int) else pl.multiple_of(start, 16)


class Transfers:
    def __init__(self, send_sem, recv_sem):
        self.send_sem, self.recv_sem = send_sem, recv_sem
        self.slots, self.made, self.waited, self.started = {}, {}, set(), []

    def declare(self, name, source, target, landed, device):
        slot = self.slots.setdefault(name, len(self.slots))

        def descriptor(dst):
            return pltpu.make_async_remote_copy(
                src_ref=source(),
                dst_ref=dst(),
                send_sem=self.send_sem.at[slot],
                recv_sem=self.recv_sem.at[slot],
                device_id=device,
                device_id_type=MESH,
            )

        self.made[name] = (descriptor, target, landed)

    def start(self, name):
        descriptor, target, _ = self.made[name]
        descriptor(target).start()
        self.started.append(name)

    def arrived(self, name):
        if name not in self.waited:
            self.waited.add(name)
            descriptor, _, landed = self.made[name]
            descriptor(landed).wait_recv()

    def drain(self):
        for name in self.started:
            descriptor, target, _ = self.made[name]
            descriptor(target).wait_send()


class Plan:
    def __init__(self, transfers):
        self.transfers = transfers
        self.tasks = []

    def send(self, name, link, load, needs=(), prepare=None, cost=0.0):
        self.tasks.append((name, link, load, tuple(needs), prepare, cost))

    def compute(self, name, cost, needs, emit):
        self.tasks.append((name, None, 0, tuple(needs), emit, cost))

    def run(self, order):
        for at in order:
            name, link, _, needs, emit, _ = self.tasks[at]
            for need in needs:
                if need in self.transfers.made:
                    self.transfers.arrived(need)
            if emit is not None:
                emit()
            if link is not None:
                self.transfers.start(name)


def kernel(
    acts_hbm,
    weights_ref,
    momentum_hbm,
    dout_ref,
    near_ref,
    far_ref,
    grad_ref,
    stepped_ref,
    acts,
    acts_t,
    momentum,
    wall,
    dout_all,
    query_all,
    keys,
    values,
    expo_buf,
    slope_buf,
    dprob_buf,
    sums_own,
    sums_in,
    inv_buf,
    delta_buf,
    dq_buf,
    dq_out,
    dq_in,
    dk_acc,
    dv_acc,
    dkv_out,
    dkv_in,
    dproj,
    own_out,
    own_in,
    pair_out,
    pair_in,
    share_out,
    share_in,
    z_out,
    z_in,
    terms,
    send_sem,
    recv_sem,
    local_sem,
):
    rows = weights_ref.shape[0]
    tokens, head = dout_ref.shape
    width = acts.shape[1]
    share = rows // 9 * 2
    kept = rows - share
    qscale = float(width // HEADS) ** (-0.5)
    pscale = float(width) ** (-0.5)
    rep = lax.axis_index("rep")
    place = lax.axis_index("fsdp")
    y = lax.div(place, 2)
    zh = lax.rem(place, 2)

    def around(step):
        return lax.rem(y + step % RING, RING)

    def column(step):
        return (rep, around(step) * 2 + zh)

    pair = (rep, y * 2 + (1 - zh))

    acts_copy = pltpu.make_async_copy(acts_hbm, acts, local_sem.at[0])
    acts_copy.start()
    momentum_copy = pltpu.make_async_copy(momentum_hbm, momentum, local_sem.at[1])
    momentum_copy.start()

    barrier = pltpu.get_barrier_semaphore()
    greeted = [column(step) for step in range(1, RING)] + [pair]
    for device in greeted:
        pl.semaphore_signal(barrier, inc=1, device_id=device, device_id_type=MESH)
    for part in range(3):
        wall[part, pl.ds(aligned(place * rows), rows), :] = weights_ref[
            :, part * head : (part + 1) * head
        ].astype(BF16)
    dout_all[pl.ds(aligned(y * tokens), tokens), :] = dout_ref[...]
    pl.semaphore_wait(barrier, len(greeted))

    moves = Transfers(send_sem, recv_sem)
    ways = ((0, 1, "up"), (1, -1, "down"))

    def gather(plan, tag, view, count, needs_of, strides=False):
        for hop in range(1, FAR + 1):
            for way, sign, link in ways:
                low, high = 0, count
                if hop == FAR:
                    low, high = ((0, count // 2), (count // 2, count))[way]
                name = (tag, hop, way)
                jump = 2 if strides and hop % 2 == 0 else 1
                held = hop - jump
                moves.declare(
                    name,
                    functools.partial(view, -sign * held, low, high),
                    functools.partial(view, -sign * held, low, high),
                    functools.partial(view, -sign * hop, low, high),
                    column(sign * jump),
                )
                needs = [(tag, held, way)] if held else needs_of
                plan.send(name, link, jump * (high - low) * head * 2, needs)

    def hops(tag):
        return [(tag, hop, way) for hop in range(1, FAR + 1) for way in range(2)]

    plan = Plan(moves)

    def wall_view(part, z, step, low, high):
        start = (around(step) * 2 + z) * rows + low
        return wall.at[part, pl.ds(aligned(start), high - low), :]

    arrivals = []
    for part in range(3):
        mine = functools.partial(wall_view, part, zh)
        theirs = functools.partial(wall_view, part, 1 - zh)
        first = ("first", part)
        moves.declare(
            first,
            functools.partial(mine, 0, 0, kept),
            functools.partial(mine, 0, 0, kept),
            functools.partial(theirs, 0, 0, kept),
            pair,
        )
        plan.send(first, "z", kept * head * 2)
        gather(plan, ("own", part), mine, rows, ())
        gather(plan, ("pair", part), theirs, kept, [first])
        names = hops(("own", part)) + hops(("pair", part)) + [first]
        passed = [(0, 0, 0)] + [
            (-sign * hop, hop, way)
            for hop in range(1, FAR + 1)
            for way, sign, _ in ways
            if hop < FAR or way == 1
        ]
        for step, hop, way in passed:
            name = ("share", part, step)
            moves.declare(
                name,
                functools.partial(mine, step, kept, rows),
                functools.partial(mine, step, kept, rows),
                functools.partial(theirs, step, kept, rows),
                pair,
            )
            needs = [] if hop == 0 else [(("own", part), hop, way)]
            plan.send(name, "z", share * head * 2, needs)
            names.append(name)
        arrivals.append(names)

    def block_view(buffer, step, low, high):
        return buffer.at[pl.ds(aligned(around(step) * tokens + low), high - low), :]

    gather(plan, "dout", functools.partial(block_view, dout_all), tokens, ())
    gather(plan, "query", functools.partial(block_view, query_all), tokens, ["query"], True)

    half_head = head // 2
    far_cos = far_ref[0, pl.ds(place, 1), :]
    far_sin = far_ref[1, pl.ds(place, 1), :]

    def turned_by(matrix, direction):
        near_cos, near_sin = near_ref[0], near_ref[1]
        cosine = near_cos * far_cos - near_sin * far_sin
        sine = near_sin * far_cos + near_cos * far_sin
        lane = lax.broadcasted_iota(jnp.int32, (tokens, head), 1)
        signed = jnp.where(lane < half_head, -sine, sine)
        return matrix * cosine + direction * pltpu.roll(matrix, half_head, 1) * signed

    here = pl.ds(aligned(y * tokens), tokens)
    mine_rows = pl.ds(aligned(zh * tokens), tokens)
    their_rows = pl.ds(aligned((1 - zh) * tokens), tokens)

    def projected(part):
        return dot_nn(acts[...], wall[part]) * pscale

    def make_query():
        query_all[here, :] = turned_by(projected(0), 1.0).astype(BF16)

    def make_keys():
        keys[mine_rows, :] = turned_by(projected(1), 1.0).astype(BF16)

    def make_values():
        values[mine_rows, :] = projected(2).astype(BF16)

    tile = 128
    tiles = width // tile
    turns = 12

    def turn(at):
        @pl.loop(at * tiles // turns, (at + 1) * tiles // turns)
        def _(t):
            at = pl.multiple_of(t * tile, tile)
            acts_t[pl.ds(at, tile), :] = acts[:, pl.ds(at, tile)].T

    plan.compute("acts", 0.1, (), acts_copy.wait)
    for at in range(turns):
        plan.compute(("turn", at), 0.25, ["acts"], functools.partial(turn, at))
    plan.compute("query", 1.0, arrivals[0] + ["acts"], make_query)
    for tag, buffer, made in (("keys", keys, make_keys), ("values", values, make_values)):
        part = 1 if tag == "keys" else 2
        plan.compute(tag, 0.9, arrivals[part] + ["acts"], made)
        moves.declare(
            (tag, "z"),
            functools.partial(lambda ref: ref.at[mine_rows, :], buffer),
            functools.partial(lambda ref: ref.at[mine_rows, :], buffer),
            functools.partial(lambda ref: ref.at[their_rows, :], buffer),
            pair,
        )
        plan.send((tag, "z"), "z", tokens * head * 2, [tag])
    plan.run(GATHER_ORDER)

    for name in hops("query") + [("keys", "z")]:
        moves.arrived(name)
    sub = min(128, 2 * tokens)
    sums_own[...] = jnp.zeros_like(sums_own)

    @pl.loop(y, RING)
    def _(block):
        query = query_all[pl.ds(aligned(block * tokens), tokens), :]
        total = jnp.zeros((1, tokens), F32)
        for low in range(0, 2 * tokens, sub):
            span = slice(low, low + sub)
            score = dot_nt(keys[span, :], query)
            tangent = jnp.tanh(score * (qscale / SOFT_CAP))
            key_at = lax.broadcasted_iota(jnp.int32, (sub, tokens), 0) + low
            query_at = lax.broadcasted_iota(jnp.int32, (sub, tokens), 1)
            keep = key_at - query_at <= (block - y) * (2 * tokens) + zh * tokens
            expo = jnp.where(keep, jnp.exp(SOFT_CAP * tangent), 0.0)
            expo_buf[block, span, :] = expo
            slope_buf[block, span, :] = expo * (1.0 - tangent * tangent)
            total += jnp.sum(expo, axis=0, keepdims=True)
        sums_own[0, pl.ds(block, 1), :] = total

    def exchange(kind):
        for step in range(1, RING):
            name = ("sums", kind, step)
            moves.declare(
                name,
                lambda: sums_own.at[kind],
                functools.partial(lambda at: sums_in.at[kind, at], step),
                functools.partial(lambda at: sums_in.at[kind, at], step),
                column(step),
            )
            moves.start(name)

    def summed(kind):
        total = sums_own[kind]
        for step in range(1, RING):
            moves.arrived(("sums", kind, step))
            total += sums_in[kind, step]
        return total

    exchange(0)
    for name in hops("dout") + [("values", "z")]:
        moves.arrived(name)

    @pl.loop(y, RING)
    def _(block):
        dout = dout_all[pl.ds(aligned(block * tokens), tokens), :]
        cross = jnp.zeros((1, tokens), F32)
        for low in range(0, 2 * tokens, sub):
            span = slice(low, low + sub)
            dprob = dot_nt(values[span, :], dout)
            dprob_buf[block, span, :] = dprob
            cross += jnp.sum(expo_buf[block, span, :] * dprob, axis=0, keepdims=True)
        sums_own[1, pl.ds(block, 1), :] = cross

    exchange(1)
    dq_buf[...] = jnp.zeros_like(dq_buf)
    dk_acc[...] = jnp.zeros_like(dk_acc)
    dv_acc[...] = jnp.zeros_like(dv_acc)
    inverse = 1.0 / summed(0)
    inv_buf[...] = inverse

    @pl.loop(y, RING)
    def _(block):
        dout = dout_all[pl.ds(aligned(block * tokens), tokens), :]
        inv = inv_buf[pl.ds(block, 1), :]
        for low in range(0, 2 * tokens, sub):
            span = slice(low, low + sub)
            dv_acc[span, :] += dot_nn((expo_buf[block, span, :] * inv).astype(BF16), dout)

    def swap(kind, acc):
        dkv_out[kind] = acc[their_rows, :].astype(BF16)
        moves.declare(
            ("swap", kind),
            lambda: dkv_out.at[kind],
            lambda: dkv_in.at[kind],
            lambda: dkv_in.at[kind],
            pair,
        )
        moves.start(("swap", kind))

    swap(1, dv_acc)
    delta_buf[...] = summed(1) * inverse

    @pl.loop(y, RING)
    def _(block):
        at = pl.ds(aligned(block * tokens), tokens)
        query = query_all[at, :]
        inv = inv_buf[pl.ds(block, 1), :] * qscale
        delta = delta_buf[pl.ds(block, 1), :]
        dquery = jnp.zeros((tokens, head), F32)
        for low in range(0, 2 * tokens, sub):
            span = slice(low, low + sub)
            dscore = slope_buf[block, span, :] * (dprob_buf[block, span, :] - delta) * inv
            dscore = dscore.astype(BF16)
            dk_acc[span, :] += dot_nn(dscore, query)
            dquery += dot_tn(dscore, keys[span, :])
        dq_buf[at, :] = dquery

    swap(0, dk_acc)

    plan = Plan(moves)

    def pieces(low, high, value, added, store):
        edges = {low, high}
        for ref, start, stop in added:
            edges |= {edge for edge in (start, stop) if low < edge < high}
        edges = sorted(edges)
        for start, stop in zip(edges[:-1], edges[1:]):
            total = value[start - low : stop - low]
            for ref, first, last in added:
                if first <= start and stop <= last:
                    total += ref[start - first : stop - first, :].astype(F32)
            store(start, stop, total)

    def chain(tag, term, extra, outgoing, incoming, count, needs_of, strides=False):
        for step in range(FAR):
            for way, sign, link in ways:
                half = ((0, count // 2), (count // 2, count))[way]
                low, high = half if step == 0 else (0, count)
                name = (tag, step, way)
                offset = (sign * (FAR - step)) % RING
                jump = 2 if strides and step % 2 == 0 else 1
                if strides:
                    inputs = [0, 1] if step == 2 else []
                else:
                    inputs = [step - 1] if step else []

                def prepare(
                    step=step, way=way, low=low, high=high, offset=offset, inputs=inputs, half=half
                ):
                    added = list(extra(offset))
                    for earlier in inputs:
                        first, last = (0, count) if earlier else half
                        added.append((incoming.at[earlier, way], first, last))

                    def store(start, stop, total):
                        outgoing[step, way, start - low : stop - low, :] = total.astype(BF16)

                    pieces(low, high, term(offset, low, high), added, store)

                def view(ref, step=step, way=way, size=high - low):
                    return ref.at[step, way, pl.ds(0, size), :]

                moves.declare(
                    name,
                    functools.partial(view, outgoing),
                    functools.partial(view, incoming),
                    functools.partial(view, incoming),
                    column(sign * jump),
                )
                needs = list(needs_of(offset, low, high))
                needs += [(tag, earlier, way) for earlier in inputs]
                plan.send(name, link, jump * (high - low) * head * 2, needs, prepare, 0.1)

    def last_hops(tag):
        return [(tag, FAR - 1, way) for way in range(2)]

    def dq_term(offset, low, high):
        start = around(offset) * tokens + low
        return dq_buf[pl.ds(aligned(start), high - low), :]

    chain(
        "dquery",
        dq_term,
        lambda offset: (),
        dq_out,
        dq_in,
        tokens,
        lambda *a: (),
        True,
    )

    def finish_dv():
        dproj[2] = (dv_acc[mine_rows, :] + dkv_in[1].astype(F32)).astype(BF16)

    def finish_dk():
        total = dk_acc[mine_rows, :] + dkv_in[0].astype(F32)
        dproj[1] = turned_by(total, -1.0).astype(BF16)

    def finish_dq():
        total = dq_buf[here, :]
        for way in range(2):
            total += dq_in[2, way].astype(F32) + dq_in[3, way].astype(F32)
        dproj[0] = turned_by(total, -1.0).astype(BF16)

    plan.compute(("dproj", 2), 0.2, [("swap", 1)], finish_dv)
    plan.compute(("dproj", 1), 0.3, [("swap", 0)], finish_dk)
    plan.compute(("dproj", 0), 0.4, [("dquery", step, way) for step in (2, 3) for way in range(2)], finish_dq)

    for part in (2, 1, 0):
        ready = ("terms", part)

        def multiply(part=part):
            size = width // 9

            @pl.loop(0, 9)
            def _(at):
                span = pl.ds(pl.multiple_of(at * size, 16), size)
                terms[part, span, :] = dot_nn(acts_t[span, :], dproj[part]) * pscale

        plan.compute(ready, 0.8, [("dproj", part)], multiply)

        def term(z, offset, low, high, part=part):
            start = (around(offset) * 2 + z) * rows + low
            return terms[part, pl.ds(aligned(start), high - low), :]

        own_term = functools.partial(term, zh)
        pair_term = functools.partial(term, 1 - zh)

        for group, (low_at, high_at) in enumerate(GROUPS):

            def hand_over(low_at=low_at, high_at=high_at, pair_term=pair_term, part=part):
                for at in range(low_at, high_at):
                    share_out[part, at] = pair_term(OFFSETS[at], kept, rows).astype(BF16)

            def span_of(ref, part=part, low_at=low_at, count=high_at - low_at):
                return ref.at[part, pl.ds(low_at, count)]

            moves.declare(
                ("handed", part, group),
                functools.partial(span_of, share_out),
                functools.partial(span_of, share_in),
                functools.partial(span_of, share_in),
                pair,
            )
            plan.send(
                ("handed", part, group),
                "z",
                (high_at - low_at) * share * head * 2,
                [ready],
                hand_over,
                0.15,
            )

        def own_extra(offset, part=part):
            return [(share_in.at[part, OFFSETS.index(offset)], kept, rows)]

        def own_needs(offset, low, high, part=part, ready=ready):
            if high <= kept:
                return [ready]
            at = OFFSETS.index(offset)
            group = [low_at <= at < high_at for low_at, high_at in GROUPS].index(True)
            return [ready, ("handed", part, group)]

        chain(
            ("gpair", part),
            pair_term,
            lambda offset: (),
            pair_out.at[part],
            pair_in.at[part],
            kept,
            lambda *a, ready=ready: [ready],
        )
        chain(
            ("gown", part),
            own_term,
            own_extra,
            own_out.at[part],
            own_in.at[part],
            rows,
            own_needs,
        )

        def settle(pair_term=pair_term, part=part):
            added = [(pair_in.at[part, FAR - 1, way], 0, kept) for way in range(2)]

            def store(start, stop, total):
                z_out[part, start:stop, :] = total.astype(BF16)

            pieces(0, kept, pair_term(0, 0, kept), added, store)

        moves.declare(
            ("settled", part),
            functools.partial(lambda at: z_out.at[at], part),
            functools.partial(lambda at: z_in.at[at], part),
            functools.partial(lambda at: z_in.at[at], part),
            pair,
        )
        plan.send(
            ("settled", part),
            "z",
            kept * head * 2,
            last_hops(("gpair", part)),
            settle,
            0.1,
        )

        def update(own_term=own_term, own_extra=own_extra, part=part):
            added = list(own_extra(0)) + [(z_in.at[part], 0, kept)]
            added += [(own_in.at[part, FAR - 1, way], 0, rows) for way in range(2)]
            lanes = slice(part * head, (part + 1) * head)

            def store(start, stop, total):
                moved = MOMENTUM_DECAY * momentum[start:stop, lanes] + total
                stepped = weights_ref[start:stop, lanes] - LEARNING_RATE * moved
                grad_ref[start:stop, lanes] = total
                stepped_ref[start:stop, lanes] = stepped.astype(BF16)

            pieces(0, rows, own_term(0, 0, rows), added, store)

        plan.compute(
            ("update", part),
            0.2,
            last_hops(("gown", part)) + [("settled", part), ("handed", part, 2), "momentum"],
            update,
        )

    plan.compute("momentum", 0.1, (), momentum_copy.wait)
    plan.run(SCATTER_ORDER)
    moves.drain()


def rope_tables(tokens, places, head):
    half = head // 2
    freqs = ROPE_BASE ** (-(np.arange(half, dtype=np.float64) * 2.0 / head))
    freqs = np.concatenate([freqs, freqs])
    near = np.arange(tokens, dtype=np.float64)[:, None] * freqs
    far = (np.arange(places, dtype=np.float64) * tokens)[:, None] * freqs
    return (
        np.stack([np.cos(near), np.sin(near)]).astype(np.float32),
        np.stack([np.cos(far), np.sin(far)]).astype(np.float32),
    )


def passed_along(value, axis, steps):
    count = lax.axis_size(axis)
    pairs = [(source, (source + steps) % count) for source in range(count)]
    return lax.ppermute(value, axis, pairs)


def on_device(activations, weights, momentum, cotangent, step):
    acts = activations[0]
    params = weights[0]
    moment = momentum[0]
    dout = cotangent[0]
    tokens, width = acts.shape
    rows, columns = params.shape
    head = dout.shape[1]
    share = rows // 9 * 2
    kept = rows - share
    near, far = rope_tables(tokens, lax.axis_size("fsdp"), head)
    near, far = jnp.asarray(near), jnp.asarray(far)
    vmem = pl.BlockSpec(memory_space=pltpu.VMEM)
    anywhere = pl.BlockSpec(memory_space=pl.ANY)
    grad, stepped = pl.pallas_call(
        kernel,
        out_shape=[
            jax.ShapeDtypeStruct((rows, columns), F32),
            jax.ShapeDtypeStruct((rows, columns), BF16),
        ],
        in_specs=[anywhere, vmem, anywhere, vmem, vmem, vmem],
        out_specs=[vmem, vmem],
        scratch_shapes=[
            pltpu.VMEM((tokens, width), BF16),
            pltpu.VMEM((width, tokens), BF16),
            pltpu.VMEM((rows, columns), F32),
            pltpu.VMEM((3, width, head), BF16),
            pltpu.VMEM((RING * tokens, head), BF16),
            pltpu.VMEM((RING * tokens, head), BF16),
            pltpu.VMEM((2 * tokens, head), BF16),
            pltpu.VMEM((2 * tokens, head), BF16),
            pltpu.VMEM((RING, 2 * tokens, tokens), F32),
            pltpu.VMEM((RING, 2 * tokens, tokens), F32),
            pltpu.VMEM((RING, 2 * tokens, tokens), F32),
            pltpu.VMEM((2, RING, tokens), F32),
            pltpu.VMEM((2, RING, RING, tokens), F32),
            pltpu.VMEM((RING, tokens), F32),
            pltpu.VMEM((RING, tokens), F32),
            pltpu.VMEM((RING * tokens, head), F32),
            pltpu.VMEM((FAR, 2, tokens, head), BF16),
            pltpu.VMEM((FAR, 2, tokens, head), BF16),
            pltpu.VMEM((2 * tokens, head), F32),
            pltpu.VMEM((2 * tokens, head), F32),
            pltpu.VMEM((2, tokens, head), BF16),
            pltpu.VMEM((2, tokens, head), BF16),
            pltpu.VMEM((3, tokens, head), BF16),
            pltpu.VMEM((3, FAR, 2, rows, head), BF16),
            pltpu.VMEM((3, FAR, 2, rows, head), BF16),
            pltpu.VMEM((3, FAR, 2, kept, head), BF16),
            pltpu.VMEM((3, FAR, 2, kept, head), BF16),
            pltpu.VMEM((3, RING, share, head), BF16),
            pltpu.VMEM((3, RING, share, head), BF16),
            pltpu.VMEM((3, kept, head), BF16),
            pltpu.VMEM((3, kept, head), BF16),
            pltpu.VMEM((3, width, head), F32),
            pltpu.SemaphoreType.DMA((SEMS,)),
            pltpu.SemaphoreType.DMA((SEMS,)),
            pltpu.SemaphoreType.DMA((2,)),
        ],
        compiler_params=pltpu.CompilerParams(
            collective_id=0, has_side_effects=True, vmem_limit_bytes=56 * 2**20
        ),
        name="attention_step",
    )(acts, params, moment, dout, near, far)
    replicas = lax.axis_size("rep")
    branches = [
        functools.partial(passed_along, axis="rep", steps=2**level % replicas)
        for level in range(PERIOD)
    ]
    partner = lax.switch(step[0] % PERIOD, branches, stepped).astype(F32)
    new_moment = MOMENTUM_DECAY * moment + grad
    new_weights = (params - LEARNING_RATE * new_moment + partner) * 0.5
    return (new_weights[None], new_moment[None])


def solution(mesh):
    spec = P("rep", "fsdp", None)
    return jax.shard_map(
        on_device,
        mesh=mesh,
        in_specs=(spec, spec, spec, spec, P()),
        out_specs=(spec, spec),
        check_vma=False,
    )
```

```python
import functools

import jax
import jax.numpy as jnp
import numpy as np
from jax import lax
from jax.experimental import pallas as pl
from jax.experimental.pallas import tpu as pltpu
from jax.sharding import PartitionSpec as P

HEADS = 32
PERIOD = 4
SOFT_CAP = 50.0
ROPE_BASE = 10000.0
MOMENTUM_DECAY = 0.9
LEARNING_RATE = 0.5
RING = 8
FAR = RING // 2
GATHER_SHARE = 3
SCATTER_SHARE = 3
STRIDES = True
BF16 = jnp.bfloat16
F32 = jnp.float32
MESH = pl.DeviceIdType.MESH
SEMS = 192
OFFSETS = (4, 3, 5, 2, 6, 1, 7, 0)
GROUPS = ((0, 3), (3, 5), (5, 8))

GATHER_ORDER = (
    0, 2, 26, 91, 95, 99, 98, 97, 51, 52, 50, 103, 102, 93, 94, 27, 1, 100, 92, 101,
    25, 96, 76, 75, 4, 19, 28, 42, 54, 9, 18, 3, 10, 17, 29, 59, 67, 21, 30, 35,
    43, 6, 34, 71, 11, 12, 20, 5, 31, 46, 47, 53, 56, 45, 61, 8, 23, 13, 37, 44,
    36, 60, 22, 7, 14, 48, 55, 33, 24, 58, 15, 73, 39, 63, 68, 62, 38, 70, 16, 77,
    78, 49, 57, 74, 41, 32, 72, 65, 64, 40, 104, 85, 86, 69, 79, 66, 105, 80, 106, 83,
    84, 89, 90, 107, 108, 81, 88, 87, 82,
)
SCATTER_ORDER = (
    1, 0, 3, 2, 8, 9, 7, 6, 79, 10, 13, 14, 5, 4, 18, 17, 16, 25, 11, 35,
    40, 39, 47, 36, 20, 19, 12, 57, 62, 26, 58, 41, 61, 42, 27, 22, 21, 64, 59, 69,
    28, 43, 44, 37, 63, 48, 49, 24, 15, 66, 23, 70, 71, 60, 46, 50, 65, 45, 38, 68,
    51, 72, 73, 30, 33, 67, 52, 29, 55, 74, 75, 32, 77, 53, 54, 31, 76, 56, 34, 78,
)


def dot_nn(left, right):
    return lax.dot_general(left, right, (((1,), (0,)), ((), ())), preferred_element_type=F32)


def dot_nt(left, right):
    return lax.dot_general(left, right, (((1,), (1,)), ((), ())), preferred_element_type=F32)


def dot_tn(left, right):
    return lax.dot_general(left, right, (((0,), (0,)), ((), ())), preferred_element_type=F32)


def aligned(start):
    return start if isinstance(start, int) else pl.multiple_of(start, 16)


class Transfers:
    def __init__(self, send_sem, recv_sem):
        self.send_sem, self.recv_sem = send_sem, recv_sem
        self.slots, self.made, self.waited, self.started = {}, {}, set(), []

    def declare(self, name, source, target, landed, device):
        slot = self.slots.setdefault(name, len(self.slots))

        def descriptor(dst):
            return pltpu.make_async_remote_copy(
                src_ref=source(),
                dst_ref=dst(),
                send_sem=self.send_sem.at[slot],
                recv_sem=self.recv_sem.at[slot],
                device_id=device,
                device_id_type=MESH,
            )

        self.made[name] = (descriptor, target, landed)

    def start(self, name):
        descriptor, target, _ = self.made[name]
        descriptor(target).start()
        self.started.append(name)

    def arrived(self, name):
        if name not in self.waited:
            self.waited.add(name)
            descriptor, _, landed = self.made[name]
            descriptor(landed).wait_recv()

    def drain(self):
        for name in self.started:
            descriptor, target, _ = self.made[name]
            descriptor(target).wait_send()


class Plan:
    def __init__(self, transfers):
        self.transfers = transfers
        self.tasks = []

    def send(self, name, link, load, needs=(), prepare=None, cost=0.0):
        self.tasks.append((name, link, load, tuple(needs), prepare, cost))

    def compute(self, name, cost, needs, emit):
        self.tasks.append((name, None, 0, tuple(needs), emit, cost))

    def run(self, order):
        for at in order:
            name, link, _, needs, emit, _ = self.tasks[at]
            for need in needs:
                if need in self.transfers.made:
                    self.transfers.arrived(need)
            if emit is not None:
                emit()
            if link is not None:
                self.transfers.start(name)


def kernel(
    acts_hbm,
    weights_ref,
    momentum_hbm,
    dout_ref,
    near_hbm,
    far_hbm,
    grad_ref,
    stepped_ref,
    acts,
    acts_t,
    momentum,
    wall,
    dout_all,
    query_all,
    keys,
    values,
    expo_buf,
    slope_buf,
    dprob_buf,
    sums_own,
    sums_in,
    inv_buf,
    delta_buf,
    dq_buf,
    dq_out,
    dq_in,
    dk_acc,
    dv_acc,
    dkv_out,
    dkv_in,
    dscore_buf,
    dproj,
    own_out,
    own_in,
    pair_out,
    pair_in,
    share_out,
    share_in,
    z_out,
    z_in,
    terms,
    near_ref,
    far_ref,
    send_sem,
    recv_sem,
    local_sem,
):
    rows = weights_ref.shape[0]
    tokens, head = dout_ref.shape
    width = acts.shape[1]
    share = rows // 9 * GATHER_SHARE
    kept = rows - share
    qscale = float(width // HEADS) ** (-0.5)
    pscale = float(width) ** (-0.5)
    rep = lax.axis_index("rep")
    place = lax.axis_index("fsdp")
    y = lax.div(place, 2)
    zh = lax.rem(place, 2)

    def around(step):
        return lax.rem(y + step % RING, RING)

    def column(step):
        return (rep, around(step) * 2 + zh)

    pair = (rep, y * 2 + (1 - zh))

    acts_copy = pltpu.make_async_copy(acts_hbm, acts, local_sem.at[0])
    acts_copy.start()
    momentum_copy = pltpu.make_async_copy(momentum_hbm, momentum, local_sem.at[1])
    momentum_copy.start()
    near_copy = pltpu.make_async_copy(near_hbm, near_ref, local_sem.at[2])
    near_copy.start()
    far_copy = pltpu.make_async_copy(far_hbm, far_ref, local_sem.at[3])
    far_copy.start()

    barrier = pltpu.get_barrier_semaphore()
    greeted = [column(step) for step in range(1, RING)] + [pair]
    for device in greeted:
        pl.semaphore_signal(barrier, inc=1, device_id=device, device_id_type=MESH)
    for part in range(3):
        wall[part, pl.ds(aligned(place * rows), rows), :] = weights_ref[
            :, part * head : (part + 1) * head
        ].astype(BF16)
    dout_all[pl.ds(aligned(y * tokens), tokens), :] = dout_ref[...]
    pl.semaphore_wait(barrier, len(greeted))

    moves = Transfers(send_sem, recv_sem)
    ways = ((0, 1, "up"), (1, -1, "down"))

    def gather(plan, tag, view, count, needs_of, strides=False):
        for hop in range(1, FAR + 1):
            for way, sign, link in ways:
                low, high = 0, count
                if hop == FAR:
                    low, high = ((0, count // 2), (count // 2, count))[way]
                name = (tag, hop, way)
                jump = 2 if strides and hop % 2 == 0 else 1
                held = hop - jump
                moves.declare(
                    name,
                    functools.partial(view, -sign * held, low, high),
                    functools.partial(view, -sign * held, low, high),
                    functools.partial(view, -sign * hop, low, high),
                    column(sign * jump),
                )
                needs = [(tag, held, way)] if held else needs_of
                plan.send(name, link, jump * (high - low) * head * 2, needs)

    def hops(tag):
        return [(tag, hop, way) for hop in range(1, FAR + 1) for way in range(2)]

    plan = Plan(moves)

    def wall_view(part, z, step, low, high):
        start = (around(step) * 2 + z) * rows + low
        return wall.at[part, pl.ds(aligned(start), high - low), :]

    arrivals = []
    for part in range(3):
        mine = functools.partial(wall_view, part, zh)
        theirs = functools.partial(wall_view, part, 1 - zh)
        first = ("first", part)
        moves.declare(
            first,
            functools.partial(mine, 0, 0, kept),
            functools.partial(mine, 0, 0, kept),
            functools.partial(theirs, 0, 0, kept),
            pair,
        )
        plan.send(first, "z", kept * head * 2)
        gather(plan, ("own", part), mine, rows, ())
        gather(plan, ("pair", part), theirs, kept, [first])
        names = hops(("own", part)) + hops(("pair", part)) + [first]
        passed = [(0, 0, 0)] + [
            (-sign * hop, hop, way)
            for hop in range(1, FAR + 1)
            for way, sign, _ in ways
            if hop < FAR or way == 1
        ]
        for step, hop, way in passed:
            name = ("share", part, step)
            moves.declare(
                name,
                functools.partial(mine, step, kept, rows),
                functools.partial(mine, step, kept, rows),
                functools.partial(theirs, step, kept, rows),
                pair,
            )
            needs = [] if hop == 0 else [(("own", part), hop, way)]
            plan.send(name, "z", share * head * 2, needs)
            names.append(name)
        arrivals.append(names)

    def block_view(buffer, step, low, high):
        return buffer.at[pl.ds(aligned(around(step) * tokens + low), high - low), :]

    gather(plan, "dout", functools.partial(block_view, dout_all), tokens, ())
    gather(plan, "query", functools.partial(block_view, query_all), tokens, ["query"], STRIDES)

    half_head = head // 2

    def turned_by(matrix, direction):
        near_cos, near_sin = near_ref[0], near_ref[1]
        far_cos, far_sin = far_ref[0, pl.ds(place, 1), :], far_ref[1, pl.ds(place, 1), :]
        cosine = near_cos * far_cos - near_sin * far_sin
        sine = near_sin * far_cos + near_cos * far_sin
        lane = lax.broadcasted_iota(jnp.int32, (tokens, head), 1)
        signed = jnp.where(lane < half_head, -sine, sine)
        return matrix * cosine + direction * pltpu.roll(matrix, half_head, 1) * signed

    here = pl.ds(aligned(y * tokens), tokens)
    mine_rows = pl.ds(aligned(zh * tokens), tokens)
    their_rows = pl.ds(aligned((1 - zh) * tokens), tokens)

    def projected(part):
        return dot_nn(acts[...], wall[part]) * pscale

    def make_query():
        query_all[here, :] = turned_by(projected(0), 1.0).astype(BF16)

    def make_keys():
        keys[mine_rows, :] = turned_by(projected(1), 1.0).astype(BF16)

    def make_values():
        values[mine_rows, :] = projected(2).astype(BF16)

    tile = 128
    tiles = width // tile
    turns = 12

    def turn(at):
        @pl.loop(at * tiles // turns, (at + 1) * tiles // turns)
        def _(t):
            at = pl.multiple_of(t * tile, tile)
            acts_t[pl.ds(at, tile), :] = acts[:, pl.ds(at, tile)].T

    def loaded():
        acts_copy.wait()
        near_copy.wait()
        far_copy.wait()

    plan.compute("acts", 0.1, (), loaded)
    for at in range(turns):
        plan.compute(("turn", at), 0.25, ["acts"], functools.partial(turn, at))
    plan.compute("query", 1.0, arrivals[0] + ["acts"], make_query)
    for tag, buffer, made in (("keys", keys, make_keys), ("values", values, make_values)):
        part = 1 if tag == "keys" else 2
        plan.compute(tag, 0.9, arrivals[part] + ["acts"], made)
        moves.declare(
            (tag, "z"),
            functools.partial(lambda ref: ref.at[mine_rows, :], buffer),
            functools.partial(lambda ref: ref.at[mine_rows, :], buffer),
            functools.partial(lambda ref: ref.at[their_rows, :], buffer),
            pair,
        )
        plan.send((tag, "z"), "z", tokens * head * 2, [tag])
    plan.run(GATHER_ORDER)

    for name in hops("query") + [("keys", "z")]:
        moves.arrived(name)
    sub = min(128, 2 * tokens)
    sums_own[...] = jnp.zeros_like(sums_own)

    @pl.loop(y, RING)
    def _(block):
        query = query_all[pl.ds(aligned(block * tokens), tokens), :]
        total = jnp.zeros((1, tokens), F32)
        for low in range(0, 2 * tokens, sub):
            span = slice(low, low + sub)
            score = dot_nt(keys[span, :], query)
            tangent = jnp.tanh(score * (qscale / SOFT_CAP))
            key_at = lax.broadcasted_iota(jnp.int32, (sub, tokens), 0) + low
            query_at = lax.broadcasted_iota(jnp.int32, (sub, tokens), 1)
            keep = key_at - query_at <= (block - y) * (2 * tokens) + zh * tokens
            expo = jnp.where(keep, jnp.exp(SOFT_CAP * tangent), 0.0)
            expo_buf[block, span, :] = expo
            slope_buf[block, span, :] = expo * (1.0 - tangent * tangent)
            total += jnp.sum(expo, axis=0, keepdims=True)
        sums_own[0, pl.ds(block, 1), :] = total

    def exchange(kind):
        for step in range(1, RING):
            name = ("sums", kind, step)
            moves.declare(
                name,
                lambda: sums_own.at[kind],
                functools.partial(lambda at: sums_in.at[kind, at], step),
                functools.partial(lambda at: sums_in.at[kind, at], step),
                column(step),
            )
            moves.start(name)

    def summed(kind):
        total = sums_own[kind]
        for step in range(1, RING):
            moves.arrived(("sums", kind, step))
            total += sums_in[kind, step]
        return total

    exchange(0)
    for name in hops("dout") + [("values", "z")]:
        moves.arrived(name)

    @pl.loop(y, RING)
    def _(block):
        dout = dout_all[pl.ds(aligned(block * tokens), tokens), :]
        cross = jnp.zeros((1, tokens), F32)
        for low in range(0, 2 * tokens, sub):
            span = slice(low, low + sub)
            dprob = dot_nt(values[span, :], dout)
            dprob_buf[block, span, :] = dprob
            cross += jnp.sum(expo_buf[block, span, :] * dprob, axis=0, keepdims=True)
        sums_own[1, pl.ds(block, 1), :] = cross

    exchange(1)
    dq_buf[...] = jnp.zeros_like(dq_buf)
    dk_acc[...] = jnp.zeros_like(dk_acc)
    dv_acc[...] = jnp.zeros_like(dv_acc)
    inverse = 1.0 / summed(0)
    inv_buf[...] = inverse

    @pl.loop(y, RING)
    def _(block):
        dout = dout_all[pl.ds(aligned(block * tokens), tokens), :]
        inv = inv_buf[pl.ds(block, 1), :]
        for low in range(0, 2 * tokens, sub):
            span = slice(low, low + sub)
            dv_acc[span, :] += dot_nn((expo_buf[block, span, :] * inv).astype(BF16), dout)

    for kind in range(2):
        moves.declare(
            ("swap", kind),
            functools.partial(lambda at: dkv_out.at[at], kind),
            functools.partial(lambda at: dkv_in.at[at], kind),
            functools.partial(lambda at: dkv_in.at[at], kind),
            pair,
        )
    dkv_out[1] = dv_acc[their_rows, :].astype(BF16)
    moves.start(("swap", 1))
    delta_buf[...] = summed(1) * inverse

    @pl.loop(y, RING)
    def _(block):
        inv = inv_buf[pl.ds(block, 1), :] * qscale
        delta = delta_buf[pl.ds(block, 1), :]
        dquery = jnp.zeros((tokens, head), F32)
        for low in range(0, 2 * tokens, sub):
            span = slice(low, low + sub)
            dscore = slope_buf[block, span, :] * (dprob_buf[block, span, :] - delta) * inv
            dscore = dscore.astype(BF16)
            dscore_buf[block, span, :] = dscore
            dquery += dot_tn(dscore, keys[span, :])
        dq_buf[pl.ds(aligned(block * tokens), tokens), :] = dquery

    def make_dk():
        @pl.loop(y, RING)
        def _(block):
            query = query_all[pl.ds(aligned(block * tokens), tokens), :]
            for low in range(0, 2 * tokens, sub):
                span = slice(low, low + sub)
                dk_acc[span, :] += dot_nn(dscore_buf[block, span, :], query)

        dkv_out[0] = dk_acc[their_rows, :].astype(BF16)

    plan = Plan(moves)

    def pieces(low, high, value, added, store):
        edges = {low, high}
        for ref, start, stop in added:
            edges |= {edge for edge in (start, stop) if low < edge < high}
        edges = sorted(edges)
        for start, stop in zip(edges[:-1], edges[1:]):
            total = value[start - low : stop - low]
            for ref, first, last in added:
                if first <= start and stop <= last:
                    total += ref[start - first : stop - first, :].astype(F32)
            store(start, stop, total)

    def chain(tag, term, extra, outgoing, incoming, count, needs_of, strides=False):
        for step in range(FAR):
            for way, sign, link in ways:
                half = ((0, count // 2), (count // 2, count))[way]
                low, high = half if step == 0 else (0, count)
                name = (tag, step, way)
                offset = (sign * (FAR - step)) % RING
                jump = 2 if strides and step % 2 == 0 else 1
                if strides:
                    inputs = [0, 1] if step == 2 else []
                else:
                    inputs = [step - 1] if step else []

                def prepare(
                    step=step, way=way, low=low, high=high, offset=offset, inputs=inputs, half=half
                ):
                    added = list(extra(offset))
                    for earlier in inputs:
                        first, last = (0, count) if earlier else half
                        added.append((incoming.at[earlier, way], first, last))

                    def store(start, stop, total):
                        outgoing[step, way, start - low : stop - low, :] = total.astype(BF16)

                    pieces(low, high, term(offset, low, high), added, store)

                def view(ref, step=step, way=way, size=high - low):
                    return ref.at[step, way, pl.ds(0, size), :]

                moves.declare(
                    name,
                    functools.partial(view, outgoing),
                    functools.partial(view, incoming),
                    functools.partial(view, incoming),
                    column(sign * jump),
                )
                needs = list(needs_of(offset, low, high))
                needs += [(tag, earlier, way) for earlier in inputs]
                plan.send(name, link, jump * (high - low) * head * 2, needs, prepare, 0.1)

    def last_hops(tag):
        return [(tag, FAR - 1, way) for way in range(2)]

    def dq_term(offset, low, high):
        start = around(offset) * tokens + low
        return dq_buf[pl.ds(aligned(start), high - low), :]

    chain(
        "dquery",
        dq_term,
        lambda offset: (),
        dq_out,
        dq_in,
        tokens,
        lambda *a: (),
        True,
    )

    def finish_dv():
        dproj[2] = (dv_acc[mine_rows, :] + dkv_in[1].astype(F32)).astype(BF16)

    def finish_dk():
        total = dk_acc[mine_rows, :] + dkv_in[0].astype(F32)
        dproj[1] = turned_by(total, -1.0).astype(BF16)

    def finish_dq():
        total = dq_buf[here, :]
        for way in range(2):
            total += dq_in[2, way].astype(F32) + dq_in[3, way].astype(F32)
        dproj[0] = turned_by(total, -1.0).astype(BF16)

    plan.compute("dk", 1.2, (), make_dk)
    plan.send(("swap", 0), "z", tokens * head * 2, ["dk"])
    plan.compute(("dproj", 2), 0.2, [("swap", 1)], finish_dv)
    plan.compute(("dproj", 1), 0.3, [("swap", 0)], finish_dk)
    plan.compute(("dproj", 0), 0.4, [("dquery", step, way) for step in (2, 3) for way in range(2)], finish_dq)

    for part in (2, 1, 0):
        ready = ("terms", part)

        def multiply(part=part):
            size = width // 9

            @pl.loop(0, 9)
            def _(at):
                span = pl.ds(pl.multiple_of(at * size, 16), size)
                terms[part, span, :] = dot_nn(acts_t[span, :], dproj[part]) * pscale

        plan.compute(ready, 0.8, [("dproj", part)], multiply)

        def term(z, offset, low, high, part=part):
            start = (around(offset) * 2 + z) * rows + low
            return terms[part, pl.ds(aligned(start), high - low), :]

        own_term = functools.partial(term, zh)
        pair_term = functools.partial(term, 1 - zh)

        for group, (low_at, high_at) in enumerate(GROUPS):

            def hand_over(low_at=low_at, high_at=high_at, pair_term=pair_term, part=part):
                for at in range(low_at, high_at):
                    share_out[part, at] = pair_term(OFFSETS[at], kept, rows).astype(BF16)

            def span_of(ref, part=part, low_at=low_at, count=high_at - low_at):
                return ref.at[part, pl.ds(low_at, count)]

            moves.declare(
                ("handed", part, group),
                functools.partial(span_of, share_out),
                functools.partial(span_of, share_in),
                functools.partial(span_of, share_in),
                pair,
            )
            plan.send(
                ("handed", part, group),
                "z",
                (high_at - low_at) * share * head * 2,
                [ready],
                hand_over,
                0.15,
            )

        def own_extra(offset, part=part):
            return [(share_in.at[part, OFFSETS.index(offset)], kept, rows)]

        def own_needs(offset, low, high, part=part, ready=ready):
            if high <= kept:
                return [ready]
            at = OFFSETS.index(offset)
            group = [low_at <= at < high_at for low_at, high_at in GROUPS].index(True)
            return [ready, ("handed", part, group)]

        chain(
            ("gpair", part),
            pair_term,
            lambda offset: (),
            pair_out.at[part],
            pair_in.at[part],
            kept,
            lambda *a, ready=ready: [ready],
        )
        chain(
            ("gown", part),
            own_term,
            own_extra,
            own_out.at[part],
            own_in.at[part],
            rows,
            own_needs,
        )

        def settle(pair_term=pair_term, part=part):
            added = [(pair_in.at[part, FAR - 1, way], 0, kept) for way in range(2)]

            def store(start, stop, total):
                z_out[part, start:stop, :] = total.astype(BF16)

            pieces(0, kept, pair_term(0, 0, kept), added, store)

        moves.declare(
            ("settled", part),
            functools.partial(lambda at: z_out.at[at], part),
            functools.partial(lambda at: z_in.at[at], part),
            functools.partial(lambda at: z_in.at[at], part),
            pair,
        )
        plan.send(
            ("settled", part),
            "z",
            kept * head * 2,
            last_hops(("gpair", part)),
            settle,
            0.1,
        )

        def update(own_term=own_term, own_extra=own_extra, part=part):
            added = list(own_extra(0)) + [(z_in.at[part], 0, kept)]
            added += [(own_in.at[part, FAR - 1, way], 0, rows) for way in range(2)]
            lanes = slice(part * head, (part + 1) * head)

            def store(start, stop, total):
                moved = MOMENTUM_DECAY * momentum[start:stop, lanes] + total
                stepped = weights_ref[start:stop, lanes] - LEARNING_RATE * moved
                grad_ref[start:stop, lanes] = total
                stepped_ref[start:stop, lanes] = stepped.astype(BF16)

            pieces(0, rows, own_term(0, 0, rows), added, store)

        plan.compute(
            ("update", part),
            0.2,
            last_hops(("gown", part)) + [("settled", part), ("handed", part, 2), "momentum"],
            update,
        )

    plan.compute("momentum", 0.1, (), momentum_copy.wait)
    plan.run(SCATTER_ORDER)
    moves.drain()


def rope_tables(tokens, places, head):
    half = head // 2
    freqs = ROPE_BASE ** (-(np.arange(half, dtype=np.float64) * 2.0 / head))
    freqs = np.concatenate([freqs, freqs])
    near = np.arange(tokens, dtype=np.float64)[:, None] * freqs
    far = (np.arange(places, dtype=np.float64) * tokens)[:, None] * freqs
    return (
        np.stack([np.cos(near), np.sin(near)]).astype(np.float32),
        np.stack([np.cos(far), np.sin(far)]).astype(np.float32),
    )


def passed_along(value, axis, steps):
    count = lax.axis_size(axis)
    pairs = [(source, (source + steps) % count) for source in range(count)]
    return lax.ppermute(value, axis, pairs)


def on_device(activations, weights, momentum, cotangent, step):
    acts = activations[0]
    params = weights[0]
    moment = momentum[0]
    dout = cotangent[0]
    tokens, width = acts.shape
    rows, columns = params.shape
    head = dout.shape[1]
    share = rows // 9 * SCATTER_SHARE
    kept = rows - share
    near, far = rope_tables(tokens, lax.axis_size("fsdp"), head)
    near, far = jnp.asarray(near), jnp.asarray(far)
    vmem = pl.BlockSpec(memory_space=pltpu.VMEM)
    anywhere = pl.BlockSpec(memory_space=pl.ANY)
    grad, stepped = pl.pallas_call(
        kernel,
        out_shape=[
            jax.ShapeDtypeStruct((rows, columns), F32),
            jax.ShapeDtypeStruct((rows, columns), BF16),
        ],
        in_specs=[anywhere, vmem, anywhere, vmem, anywhere, anywhere],
        out_specs=[vmem, vmem],
        scratch_shapes=[
            pltpu.VMEM((tokens, width), BF16),
            pltpu.VMEM((width, tokens), BF16),
            pltpu.VMEM((rows, columns), F32),
            pltpu.VMEM((3, width, head), BF16),
            pltpu.VMEM((RING * tokens, head), BF16),
            pltpu.VMEM((RING * tokens, head), BF16),
            pltpu.VMEM((2 * tokens, head), BF16),
            pltpu.VMEM((2 * tokens, head), BF16),
            pltpu.VMEM((RING, 2 * tokens, tokens), F32),
            pltpu.VMEM((RING, 2 * tokens, tokens), F32),
            pltpu.VMEM((RING, 2 * tokens, tokens), F32),
            pltpu.VMEM((2, RING, tokens), F32),
            pltpu.VMEM((2, RING, RING, tokens), F32),
            pltpu.VMEM((RING, tokens), F32),
            pltpu.VMEM((RING, tokens), F32),
            pltpu.VMEM((RING * tokens, head), F32),
            pltpu.VMEM((FAR, 2, tokens, head), BF16),
            pltpu.VMEM((FAR, 2, tokens, head), BF16),
            pltpu.VMEM((2 * tokens, head), F32),
            pltpu.VMEM((2 * tokens, head), F32),
            pltpu.VMEM((2, tokens, head), BF16),
            pltpu.VMEM((2, tokens, head), BF16),
            pltpu.VMEM((RING, 2 * tokens, tokens), BF16),
            pltpu.VMEM((3, tokens, head), BF16),
            pltpu.VMEM((3, FAR, 2, rows, head), BF16),
            pltpu.VMEM((3, FAR, 2, rows, head), BF16),
            pltpu.VMEM((3, FAR, 2, kept, head), BF16),
            pltpu.VMEM((3, FAR, 2, kept, head), BF16),
            pltpu.VMEM((3, RING, share, head), BF16),
            pltpu.VMEM((3, RING, share, head), BF16),
            pltpu.VMEM((3, kept, head), BF16),
            pltpu.VMEM((3, kept, head), BF16),
            pltpu.VMEM((3, width, head), F32),
            pltpu.VMEM(near.shape, F32),
            pltpu.VMEM(far.shape, F32),
            pltpu.SemaphoreType.DMA((SEMS,)),
            pltpu.SemaphoreType.DMA((SEMS,)),
            pltpu.SemaphoreType.DMA((4,)),
        ],
        compiler_params=pltpu.CompilerParams(
            collective_id=0, has_side_effects=True, vmem_limit_bytes=56 * 2**20
        ),
        name="attention_step",
    )(acts, params, moment, dout, near, far)
    replicas = lax.axis_size("rep")
    branches = [
        functools.partial(passed_along, axis="rep", steps=2**level % replicas)
        for level in range(PERIOD)
    ]
    partner = lax.switch(step[0] % PERIOD, branches, stepped).astype(F32)
    new_moment = MOMENTUM_DECAY * moment + grad
    new_weights = (params - LEARNING_RATE * new_moment + partner) * 0.5
    return (new_weights[None], new_moment[None])


def solution(mesh):
    spec = P("rep", "fsdp", None)
    return jax.shard_map(
        on_device,
        mesh=mesh,
        in_specs=(spec, spec, spec, spec, P()),
        out_specs=(spec, spec),
        check_vma=False,
    )
```

```python
import functools

import jax
import jax.numpy as jnp
import numpy as np
from jax import lax
from jax.experimental import pallas as pl
from jax.experimental.pallas import tpu as pltpu
from jax.sharding import PartitionSpec as P

HEADS = 32
PERIOD = 4
SOFT_CAP = 50.0
ROPE_BASE = 10000.0
MOMENTUM_DECAY = 0.9
LEARNING_RATE = 0.5
RING = 8
FAR = RING // 2
GATHER_SHARE = 3
SCATTER_SHARE = 3
STRIDES = True
BF16 = jnp.bfloat16
F32 = jnp.float32
MESH = pl.DeviceIdType.MESH
SEMS = 192
OFFSETS = (4, 3, 5, 2, 6, 1, 7, 0)
GROUPS = ((0, 3), (3, 5), (5, 8))

GATHER_ORDER = (
    0, 2, 26, 91, 95, 99, 98, 97, 51, 52, 50, 103, 102, 93, 94, 27, 1, 100, 92, 101,
    25, 96, 76, 75, 4, 19, 28, 42, 54, 9, 18, 3, 10, 17, 29, 59, 67, 21, 30, 35,
    43, 6, 34, 71, 11, 12, 20, 5, 31, 46, 47, 53, 56, 45, 61, 8, 23, 13, 37, 44,
    36, 60, 22, 7, 14, 48, 55, 33, 24, 58, 15, 73, 39, 63, 68, 62, 38, 70, 16, 77,
    78, 49, 57, 74, 41, 32, 72, 65, 64, 40, 104, 85, 86, 69, 79, 66, 105, 80, 106, 83,
    84, 89, 90, 107, 108, 81, 88, 87, 82,
)
SCATTER_ORDER = (
    1, 0, 3, 2, 8, 9, 7, 6, 79, 10, 13, 14, 5, 4, 18, 17, 16, 25, 11, 35,
    40, 39, 47, 36, 20, 19, 12, 57, 62, 26, 58, 41, 61, 42, 27, 22, 21, 64, 59, 69,
    28, 43, 44, 37, 63, 48, 49, 24, 15, 66, 23, 70, 71, 60, 46, 50, 65, 45, 38, 68,
    51, 72, 73, 30, 33, 67, 52, 29, 55, 74, 75, 32, 77, 53, 54, 31, 76, 56, 34, 78,
)


def dot_nn(left, right):
    return lax.dot_general(left, right, (((1,), (0,)), ((), ())), preferred_element_type=F32)


def dot_nt(left, right):
    return lax.dot_general(left, right, (((1,), (1,)), ((), ())), preferred_element_type=F32)


def dot_tn(left, right):
    return lax.dot_general(left, right, (((0,), (0,)), ((), ())), preferred_element_type=F32)


def aligned(start):
    return start if isinstance(start, int) else pl.multiple_of(start, 16)


class Transfers:
    def __init__(self, send_sem, recv_sem):
        self.send_sem, self.recv_sem = send_sem, recv_sem
        self.slots, self.made, self.waited, self.started = {}, {}, set(), []

    def declare(self, name, source, target, landed, device):
        slot = self.slots.setdefault(name, len(self.slots))

        def descriptor(dst):
            return pltpu.make_async_remote_copy(
                src_ref=source(),
                dst_ref=dst(),
                send_sem=self.send_sem.at[slot],
                recv_sem=self.recv_sem.at[slot],
                device_id=device,
                device_id_type=MESH,
            )

        self.made[name] = (descriptor, target, landed)

    def start(self, name):
        descriptor, target, _ = self.made[name]
        descriptor(target).start()
        self.started.append(name)

    def arrived(self, name):
        if name not in self.waited:
            self.waited.add(name)
            descriptor, _, landed = self.made[name]
            descriptor(landed).wait_recv()

    def drain(self):
        for name in self.started:
            descriptor, target, _ = self.made[name]
            descriptor(target).wait_send()


class Plan:
    def __init__(self, transfers):
        self.transfers = transfers
        self.tasks = []

    def send(self, name, link, load, needs=(), prepare=None, cost=0.0):
        self.tasks.append((name, link, load, tuple(needs), prepare, cost))

    def compute(self, name, cost, needs, emit):
        self.tasks.append((name, None, 0, tuple(needs), emit, cost))

    def run(self, order):
        for at in order:
            name, link, _, needs, emit, _ = self.tasks[at]
            for need in needs:
                if need in self.transfers.made:
                    self.transfers.arrived(need)
            if emit is not None:
                emit()
            if link is not None:
                self.transfers.start(name)


def kernel(
    acts_hbm,
    weights_ref,
    momentum_hbm,
    dout_ref,
    near_hbm,
    far_hbm,
    new_momentum_ref,
    kept_ref,
    stepped_ref,
    acts,
    acts_t,
    momentum,
    wall,
    dout_all,
    query_all,
    keys,
    values,
    expo_buf,
    slope_buf,
    dprob_buf,
    sums_own,
    sums_in,
    inv_buf,
    delta_buf,
    dq_buf,
    dq_out,
    dq_in,
    dk_acc,
    dv_acc,
    dkv_out,
    dkv_in,
    dscore_buf,
    dproj,
    own_out,
    own_in,
    pair_out,
    pair_in,
    share_out,
    share_in,
    z_out,
    z_in,
    terms,
    near_ref,
    far_ref,
    send_sem,
    recv_sem,
    local_sem,
):
    rows = weights_ref.shape[0]
    tokens, head = dout_ref.shape
    width = acts.shape[1]
    share = rows // 9 * GATHER_SHARE
    kept = rows - share
    qscale = float(width // HEADS) ** (-0.5)
    pscale = float(width) ** (-0.5)
    rep = lax.axis_index("rep")
    place = lax.axis_index("fsdp")
    y = lax.div(place, 2)
    zh = lax.rem(place, 2)

    def around(step):
        return lax.rem(y + step % RING, RING)

    def column(step):
        return (rep, around(step) * 2 + zh)

    pair = (rep, y * 2 + (1 - zh))

    acts_copy = pltpu.make_async_copy(acts_hbm, acts, local_sem.at[0])
    acts_copy.start()
    momentum_copy = pltpu.make_async_copy(momentum_hbm, momentum, local_sem.at[1])
    momentum_copy.start()
    near_copy = pltpu.make_async_copy(near_hbm, near_ref, local_sem.at[2])
    near_copy.start()
    far_copy = pltpu.make_async_copy(far_hbm, far_ref, local_sem.at[3])
    far_copy.start()

    barrier = pltpu.get_barrier_semaphore()
    greeted = [column(step) for step in range(1, RING)] + [pair]
    for device in greeted:
        pl.semaphore_signal(barrier, inc=1, device_id=device, device_id_type=MESH)
    for part in range(3):
        wall[part, pl.ds(aligned(place * rows), rows), :] = weights_ref[
            :, part * head : (part + 1) * head
        ].astype(BF16)
    dout_all[pl.ds(aligned(y * tokens), tokens), :] = dout_ref[...]
    pl.semaphore_wait(barrier, len(greeted))

    moves = Transfers(send_sem, recv_sem)
    ways = ((0, 1, "up"), (1, -1, "down"))

    def gather(plan, tag, view, count, needs_of, strides=False):
        for hop in range(1, FAR + 1):
            for way, sign, link in ways:
                low, high = 0, count
                if hop == FAR:
                    low, high = ((0, count // 2), (count // 2, count))[way]
                name = (tag, hop, way)
                jump = 2 if strides and hop % 2 == 0 else 1
                held = hop - jump
                moves.declare(
                    name,
                    functools.partial(view, -sign * held, low, high),
                    functools.partial(view, -sign * held, low, high),
                    functools.partial(view, -sign * hop, low, high),
                    column(sign * jump),
                )
                needs = [(tag, held, way)] if held else needs_of
                plan.send(name, link, jump * (high - low) * head * 2, needs)

    def hops(tag):
        return [(tag, hop, way) for hop in range(1, FAR + 1) for way in range(2)]

    plan = Plan(moves)

    def wall_view(part, z, step, low, high):
        start = (around(step) * 2 + z) * rows + low
        return wall.at[part, pl.ds(aligned(start), high - low), :]

    arrivals = []
    for part in range(3):
        mine = functools.partial(wall_view, part, zh)
        theirs = functools.partial(wall_view, part, 1 - zh)
        first = ("first", part)
        moves.declare(
            first,
            functools.partial(mine, 0, 0, kept),
            functools.partial(mine, 0, 0, kept),
            functools.partial(theirs, 0, 0, kept),
            pair,
        )
        plan.send(first, "z", kept * head * 2)
        gather(plan, ("own", part), mine, rows, ())
        gather(plan, ("pair", part), theirs, kept, [first])
        names = hops(("own", part)) + hops(("pair", part)) + [first]
        passed = [(0, 0, 0)] + [
            (-sign * hop, hop, way)
            for hop in range(1, FAR + 1)
            for way, sign, _ in ways
            if hop < FAR or way == 1
        ]
        for step, hop, way in passed:
            name = ("share", part, step)
            moves.declare(
                name,
                functools.partial(mine, step, kept, rows),
                functools.partial(mine, step, kept, rows),
                functools.partial(theirs, step, kept, rows),
                pair,
            )
            needs = [] if hop == 0 else [(("own", part), hop, way)]
            plan.send(name, "z", share * head * 2, needs)
            names.append(name)
        arrivals.append(names)

    def block_view(buffer, step, low, high):
        return buffer.at[pl.ds(aligned(around(step) * tokens + low), high - low), :]

    gather(plan, "dout", functools.partial(block_view, dout_all), tokens, ())
    gather(plan, "query", functools.partial(block_view, query_all), tokens, ["query"], STRIDES)

    half_head = head // 2

    def turned_by(matrix, direction):
        near_cos, near_sin = near_ref[0], near_ref[1]
        far_cos, far_sin = far_ref[0, pl.ds(place, 1), :], far_ref[1, pl.ds(place, 1), :]
        cosine = near_cos * far_cos - near_sin * far_sin
        sine = near_sin * far_cos + near_cos * far_sin
        lane = lax.broadcasted_iota(jnp.int32, (tokens, head), 1)
        signed = jnp.where(lane < half_head, -sine, sine)
        return matrix * cosine + direction * pltpu.roll(matrix, half_head, 1) * signed

    here = pl.ds(aligned(y * tokens), tokens)
    mine_rows = pl.ds(aligned(zh * tokens), tokens)
    their_rows = pl.ds(aligned((1 - zh) * tokens), tokens)

    def projected(part):
        return dot_nn(acts[...], wall[part]) * pscale

    def make_query():
        query_all[here, :] = turned_by(projected(0), 1.0).astype(BF16)

    def make_keys():
        keys[mine_rows, :] = turned_by(projected(1), 1.0).astype(BF16)

    def make_values():
        values[mine_rows, :] = projected(2).astype(BF16)

    tile = 128
    tiles = width // tile
    turns = 12

    def turn(at):
        @pl.loop(at * tiles // turns, (at + 1) * tiles // turns)
        def _(t):
            at = pl.multiple_of(t * tile, tile)
            acts_t[pl.ds(at, tile), :] = acts[:, pl.ds(at, tile)].T

    def loaded():
        acts_copy.wait()
        near_copy.wait()
        far_copy.wait()

    plan.compute("acts", 0.1, (), loaded)
    for at in range(turns):
        plan.compute(("turn", at), 0.25, ["acts"], functools.partial(turn, at))
    plan.compute("query", 1.0, arrivals[0] + ["acts"], make_query)
    for tag, buffer, made in (("keys", keys, make_keys), ("values", values, make_values)):
        part = 1 if tag == "keys" else 2
        plan.compute(tag, 0.9, arrivals[part] + ["acts"], made)
        moves.declare(
            (tag, "z"),
            functools.partial(lambda ref: ref.at[mine_rows, :], buffer),
            functools.partial(lambda ref: ref.at[mine_rows, :], buffer),
            functools.partial(lambda ref: ref.at[their_rows, :], buffer),
            pair,
        )
        plan.send((tag, "z"), "z", tokens * head * 2, [tag])
    plan.run(GATHER_ORDER)

    for name in hops("query") + [("keys", "z")]:
        moves.arrived(name)
    sub = min(128, 2 * tokens)
    sums_own[...] = jnp.zeros_like(sums_own)

    @pl.loop(y, RING)
    def _(block):
        query = query_all[pl.ds(aligned(block * tokens), tokens), :]
        total = jnp.zeros((1, tokens), F32)
        for low in range(0, 2 * tokens, sub):
            span = slice(low, low + sub)
            score = dot_nt(keys[span, :], query)
            tangent = jnp.tanh(score * (qscale / SOFT_CAP))
            key_at = lax.broadcasted_iota(jnp.int32, (sub, tokens), 0) + low
            query_at = lax.broadcasted_iota(jnp.int32, (sub, tokens), 1)
            keep = key_at - query_at <= (block - y) * (2 * tokens) + zh * tokens
            expo = jnp.where(keep, jnp.exp(SOFT_CAP * tangent), 0.0)
            expo_buf[block, span, :] = expo
            slope_buf[block, span, :] = expo * (1.0 - tangent * tangent)
            total += jnp.sum(expo, axis=0, keepdims=True)
        sums_own[0, pl.ds(block, 1), :] = total

    def exchange(kind):
        for step in OFFSETS[:-1]:
            name = ("sums", kind, step)
            moves.declare(
                name,
                lambda: sums_own.at[kind],
                functools.partial(lambda at: sums_in.at[kind, at], step),
                functools.partial(lambda at: sums_in.at[kind, at], step),
                column(step),
            )
            moves.start(name)

    def summed(kind):
        total = sums_own[kind]
        for step in range(1, RING):
            moves.arrived(("sums", kind, step))
            total += sums_in[kind, step]
        return total

    exchange(0)
    for name in hops("dout") + [("values", "z")]:
        moves.arrived(name)

    @pl.loop(y, RING)
    def _(block):
        dout = dout_all[pl.ds(aligned(block * tokens), tokens), :]
        cross = jnp.zeros((1, tokens), F32)
        for low in range(0, 2 * tokens, sub):
            span = slice(low, low + sub)
            dprob = dot_nt(values[span, :], dout)
            dprob_buf[block, span, :] = dprob
            cross += jnp.sum(expo_buf[block, span, :] * dprob, axis=0, keepdims=True)
        sums_own[1, pl.ds(block, 1), :] = cross

    exchange(1)
    dq_buf[...] = jnp.zeros_like(dq_buf)
    dk_acc[...] = jnp.zeros_like(dk_acc)
    dv_acc[...] = jnp.zeros_like(dv_acc)
    inverse = 1.0 / summed(0)
    inv_buf[...] = inverse

    @pl.loop(y, RING)
    def _(block):
        dout = dout_all[pl.ds(aligned(block * tokens), tokens), :]
        inv = inv_buf[pl.ds(block, 1), :]
        for low in range(0, 2 * tokens, sub):
            span = slice(low, low + sub)
            dv_acc[span, :] += dot_nn((expo_buf[block, span, :] * inv).astype(BF16), dout)

    for kind in range(2):
        moves.declare(
            ("swap", kind),
            functools.partial(lambda at: dkv_out.at[at], kind),
            functools.partial(lambda at: dkv_in.at[at], kind),
            functools.partial(lambda at: dkv_in.at[at], kind),
            pair,
        )
    dkv_out[1] = dv_acc[their_rows, :].astype(BF16)
    moves.start(("swap", 1))
    delta_buf[...] = summed(1) * inverse

    @pl.loop(y, RING)
    def _(block):
        inv = inv_buf[pl.ds(block, 1), :] * qscale
        delta = delta_buf[pl.ds(block, 1), :]
        dquery = jnp.zeros((tokens, head), F32)
        for low in range(0, 2 * tokens, sub):
            span = slice(low, low + sub)
            dscore = slope_buf[block, span, :] * (dprob_buf[block, span, :] - delta) * inv
            dscore = dscore.astype(BF16)
            dscore_buf[block, span, :] = dscore
            dquery += dot_tn(dscore, keys[span, :])
        dq_buf[pl.ds(aligned(block * tokens), tokens), :] = dquery

    def make_dk():
        @pl.loop(y, RING)
        def _(block):
            query = query_all[pl.ds(aligned(block * tokens), tokens), :]
            for low in range(0, 2 * tokens, sub):
                span = slice(low, low + sub)
                dk_acc[span, :] += dot_nn(dscore_buf[block, span, :], query)

        dkv_out[0] = dk_acc[their_rows, :].astype(BF16)

    plan = Plan(moves)

    def pieces(low, high, value, added, store):
        edges = {low, high}
        for ref, start, stop in added:
            edges |= {edge for edge in (start, stop) if low < edge < high}
        edges = sorted(edges)
        for start, stop in zip(edges[:-1], edges[1:]):
            total = value[start - low : stop - low]
            for ref, first, last in added:
                if first <= start and stop <= last:
                    total += ref[start - first : stop - first, :].astype(F32)
            store(start, stop, total)

    def chain(tag, term, extra, outgoing, incoming, count, needs_of, strides=False):
        for step in range(FAR):
            for way, sign, link in ways:
                half = ((0, count // 2), (count // 2, count))[way]
                low, high = half if step == 0 else (0, count)
                name = (tag, step, way)
                offset = (sign * (FAR - step)) % RING
                jump = 2 if strides and step % 2 == 0 else 1
                if strides:
                    inputs = [0, 1] if step == 2 else []
                else:
                    inputs = [step - 1] if step else []

                def prepare(
                    step=step, way=way, low=low, high=high, offset=offset, inputs=inputs, half=half
                ):
                    added = list(extra(offset))
                    for earlier in inputs:
                        first, last = (0, count) if earlier else half
                        added.append((incoming.at[earlier, way], first, last))

                    def store(start, stop, total):
                        outgoing[step, way, start - low : stop - low, :] = total.astype(BF16)

                    pieces(low, high, term(offset, low, high), added, store)

                def view(ref, step=step, way=way, size=high - low):
                    return ref.at[step, way, pl.ds(0, size), :]

                moves.declare(
                    name,
                    functools.partial(view, outgoing),
                    functools.partial(view, incoming),
                    functools.partial(view, incoming),
                    column(sign * jump),
                )
                needs = list(needs_of(offset, low, high))
                needs += [(tag, earlier, way) for earlier in inputs]
                plan.send(name, link, jump * (high - low) * head * 2, needs, prepare, 0.1)

    def last_hops(tag):
        return [(tag, FAR - 1, way) for way in range(2)]

    def dq_term(offset, low, high):
        start = around(offset) * tokens + low
        return dq_buf[pl.ds(aligned(start), high - low), :]

    chain(
        "dquery",
        dq_term,
        lambda offset: (),
        dq_out,
        dq_in,
        tokens,
        lambda *a: (),
        True,
    )

    def finish_dv():
        dproj[2] = (dv_acc[mine_rows, :] + dkv_in[1].astype(F32)).astype(BF16)

    def finish_dk():
        total = dk_acc[mine_rows, :] + dkv_in[0].astype(F32)
        dproj[1] = turned_by(total, -1.0).astype(BF16)

    def finish_dq():
        total = dq_buf[here, :]
        for way in range(2):
            total += dq_in[2, way].astype(F32) + dq_in[3, way].astype(F32)
        dproj[0] = turned_by(total, -1.0).astype(BF16)

    plan.compute("dk", 1.2, (), make_dk)
    plan.send(("swap", 0), "z", tokens * head * 2, ["dk"])
    plan.compute(("dproj", 2), 0.2, [("swap", 1)], finish_dv)
    plan.compute(("dproj", 1), 0.3, [("swap", 0)], finish_dk)
    plan.compute(("dproj", 0), 0.4, [("dquery", step, way) for step in (2, 3) for way in range(2)], finish_dq)

    for part in (2, 1, 0):
        ready = ("terms", part)

        def multiply(part=part):
            size = width // 9

            @pl.loop(0, 9)
            def _(at):
                span = pl.ds(pl.multiple_of(at * size, 16), size)
                terms[part, span, :] = dot_nn(acts_t[span, :], dproj[part]) * pscale

        plan.compute(ready, 0.8, [("dproj", part)], multiply)

        def term(z, offset, low, high, part=part):
            start = (around(offset) * 2 + z) * rows + low
            return terms[part, pl.ds(aligned(start), high - low), :]

        own_term = functools.partial(term, zh)
        pair_term = functools.partial(term, 1 - zh)

        for group, (low_at, high_at) in enumerate(GROUPS):

            def hand_over(low_at=low_at, high_at=high_at, pair_term=pair_term, part=part):
                for at in range(low_at, high_at):
                    share_out[part, at] = pair_term(OFFSETS[at], kept, rows).astype(BF16)

            def span_of(ref, part=part, low_at=low_at, count=high_at - low_at):
                return ref.at[part, pl.ds(low_at, count)]

            moves.declare(
                ("handed", part, group),
                functools.partial(span_of, share_out),
                functools.partial(span_of, share_in),
                functools.partial(span_of, share_in),
                pair,
            )
            plan.send(
                ("handed", part, group),
                "z",
                (high_at - low_at) * share * head * 2,
                [ready],
                hand_over,
                0.15,
            )

        def own_extra(offset, part=part):
            return [(share_in.at[part, OFFSETS.index(offset)], kept, rows)]

        def own_needs(offset, low, high, part=part, ready=ready):
            if high <= kept:
                return [ready]
            at = OFFSETS.index(offset)
            group = [low_at <= at < high_at for low_at, high_at in GROUPS].index(True)
            return [ready, ("handed", part, group)]

        chain(
            ("gpair", part),
            pair_term,
            lambda offset: (),
            pair_out.at[part],
            pair_in.at[part],
            kept,
            lambda *a, ready=ready: [ready],
        )
        chain(
            ("gown", part),
            own_term,
            own_extra,
            own_out.at[part],
            own_in.at[part],
            rows,
            own_needs,
        )

        def settle(pair_term=pair_term, part=part):
            added = [(pair_in.at[part, FAR - 1, way], 0, kept) for way in range(2)]

            def store(start, stop, total):
                z_out[part, start:stop, :] = total.astype(BF16)

            pieces(0, kept, pair_term(0, 0, kept), added, store)

        moves.declare(
            ("settled", part),
            functools.partial(lambda at: z_out.at[at], part),
            functools.partial(lambda at: z_in.at[at], part),
            functools.partial(lambda at: z_in.at[at], part),
            pair,
        )
        plan.send(
            ("settled", part),
            "z",
            kept * head * 2,
            last_hops(("gpair", part)),
            settle,
            0.1,
        )

        def update(own_term=own_term, own_extra=own_extra, part=part):
            added = list(own_extra(0)) + [(z_in.at[part], 0, kept)]
            added += [(own_in.at[part, FAR - 1, way], 0, rows) for way in range(2)]
            lanes = slice(part * head, (part + 1) * head)

            def store(start, stop, total):
                moved = MOMENTUM_DECAY * momentum[start:stop, lanes] + total
                stepped = weights_ref[start:stop, lanes] - LEARNING_RATE * moved
                new_momentum_ref[start:stop, lanes] = moved
                kept_ref[start:stop, lanes] = stepped
                stepped_ref[start:stop, lanes] = stepped.astype(BF16)

            pieces(0, rows, own_term(0, 0, rows), added, store)

        plan.compute(
            ("update", part),
            0.2,
            last_hops(("gown", part)) + [("settled", part), ("handed", part, 2), "momentum"],
            update,
        )

    plan.compute("momentum", 0.1, (), momentum_copy.wait)
    plan.run(SCATTER_ORDER)
    moves.drain()


def rope_tables(tokens, places, head):
    half = head // 2
    freqs = ROPE_BASE ** (-(np.arange(half, dtype=np.float64) * 2.0 / head))
    freqs = np.concatenate([freqs, freqs])
    near = np.arange(tokens, dtype=np.float64)[:, None] * freqs
    far = (np.arange(places, dtype=np.float64) * tokens)[:, None] * freqs
    return (
        np.stack([np.cos(near), np.sin(near)]).astype(np.float32),
        np.stack([np.cos(far), np.sin(far)]).astype(np.float32),
    )


def passed_along(value, axis, steps):
    count = lax.axis_size(axis)
    pairs = [(source, (source + steps) % count) for source in range(count)]
    return lax.ppermute(value, axis, pairs)


def on_device(activations, weights, momentum, cotangent, step):
    acts = activations[0]
    params = weights[0]
    moment = momentum[0]
    dout = cotangent[0]
    tokens, width = acts.shape
    rows, columns = params.shape
    head = dout.shape[1]
    share = rows // 9 * SCATTER_SHARE
    kept = rows - share
    near, far = rope_tables(tokens, lax.axis_size("fsdp"), head)
    near, far = jnp.asarray(near), jnp.asarray(far)
    vmem = pl.BlockSpec(memory_space=pltpu.VMEM)
    anywhere = pl.BlockSpec(memory_space=pl.ANY)
    new_moment, own_stepped, stepped = pl.pallas_call(
        kernel,
        out_shape=[
            jax.ShapeDtypeStruct((rows, columns), F32),
            jax.ShapeDtypeStruct((rows, columns), F32),
            jax.ShapeDtypeStruct((rows, columns), BF16),
        ],
        in_specs=[anywhere, vmem, anywhere, vmem, anywhere, anywhere],
        out_specs=[vmem, vmem, vmem],
        scratch_shapes=[
            pltpu.VMEM((tokens, width), BF16),
            pltpu.VMEM((width, tokens), BF16),
            pltpu.VMEM((rows, columns), F32),
            pltpu.VMEM((3, width, head), BF16),
            pltpu.VMEM((RING * tokens, head), BF16),
            pltpu.VMEM((RING * tokens, head), BF16),
            pltpu.VMEM((2 * tokens, head), BF16),
            pltpu.VMEM((2 * tokens, head), BF16),
            pltpu.VMEM((RING, 2 * tokens, tokens), F32),
            pltpu.VMEM((RING, 2 * tokens, tokens), F32),
            pltpu.VMEM((RING, 2 * tokens, tokens), F32),
            pltpu.VMEM((2, RING, tokens), F32),
            pltpu.VMEM((2, RING, RING, tokens), F32),
            pltpu.VMEM((RING, tokens), F32),
            pltpu.VMEM((RING, tokens), F32),
            pltpu.VMEM((RING * tokens, head), F32),
            pltpu.VMEM((FAR, 2, tokens, head), BF16),
            pltpu.VMEM((FAR, 2, tokens, head), BF16),
            pltpu.VMEM((2 * tokens, head), F32),
            pltpu.VMEM((2 * tokens, head), F32),
            pltpu.VMEM((2, tokens, head), BF16),
            pltpu.VMEM((2, tokens, head), BF16),
            pltpu.VMEM((RING, 2 * tokens, tokens), BF16),
            pltpu.VMEM((3, tokens, head), BF16),
            pltpu.VMEM((3, FAR, 2, rows, head), BF16),
            pltpu.VMEM((3, FAR, 2, rows, head), BF16),
            pltpu.VMEM((3, FAR, 2, kept, head), BF16),
            pltpu.VMEM((3, FAR, 2, kept, head), BF16),
            pltpu.VMEM((3, RING, share, head), BF16),
            pltpu.VMEM((3, RING, share, head), BF16),
            pltpu.VMEM((3, kept, head), BF16),
            pltpu.VMEM((3, kept, head), BF16),
            pltpu.VMEM((3, width, head), F32),
            pltpu.VMEM(near.shape, F32),
            pltpu.VMEM(far.shape, F32),
            pltpu.SemaphoreType.DMA((SEMS,)),
            pltpu.SemaphoreType.DMA((SEMS,)),
            pltpu.SemaphoreType.DMA((4,)),
        ],
        compiler_params=pltpu.CompilerParams(
            collective_id=0, has_side_effects=True, vmem_limit_bytes=56 * 2**20
        ),
        name="attention_step",
    )(acts, params, moment, dout, near, far)
    replicas = lax.axis_size("rep")
    branches = [
        functools.partial(passed_along, axis="rep", steps=2**level % replicas)
        for level in range(PERIOD)
    ]
    partner = lax.switch(step[0] % PERIOD, branches, stepped).astype(F32)
    new_weights = (own_stepped + partner) * 0.5
    return (new_weights[None], new_moment[None])


def solution(mesh):
    spec = P("rep", "fsdp", None)
    return jax.shard_map(
        on_device,
        mesh=mesh,
        in_specs=(spec, spec, spec, spec, P()),
        out_specs=(spec, spec),
        check_vma=False,
    )
```
